128 devices in a mesh: wide: 16 (over y, x_lo, core), narrow: 8 (over z, x_hi).
Axes of the slice: x: 4 (x_hi: 2, x_lo: 2; x = x_hi * 2 + x_lo), y: 4, z: 4, core: 2. Of those that a mesh axis runs over, the one named last changes fastest.
Arguments:
- interior: bfloat16 [16384, 65536], P('wide', 'narrow'), may hold values from -0.375 to 0.375
- tile_mask: int32 [256, 1024], P('wide', 'narrow'), may hold values 0 or 1
- owner: int32 [2], replicated, may hold values from 0 to 127
- stiffness: float32 [2, 512, 65536], P(None, 'wide', 'narrow'), may hold values from -4 to 4
Outputs:
- complement: float32 [2, 512, 65536], P(None, 'wide', 'narrow')
The draws below stay inside these ranges and needn't reach their ends.
All inputs are finite; a program needn't handle non-finite values. No bound on the sum of `tile_mask` on one device may be relied on, other than what follows from the above.
Results may differ from the reference program's by a relative error of at most 0.0003.
Values may be sent and summed in bfloat16 or wider, within the bound.
A program may use at most 192 MiB of HBM per device.

```python
import jax
import jax.numpy as jnp
from jax import lax

NB = 65536
PW = 512
STEPS = 2
RI_DEV = 1024
NI = 16384
N_WIDE = 16


def plant(values, own_key, low, largest):
    extent = values.shape
    index_at = [jax.random.randint(jax.random.fold_in(own_key, axis), (), 0, extent[axis]) for axis in range(len(extent))]
    values = values.at[tuple(index_at)].set(low)
    longest = extent.index(max(extent))
    index_at[longest] = (index_at[longest] + 1) % extent[longest]
    return values.at[tuple(index_at)].set(largest)


def block_levels(own_key, shape, split, least, largest):
    def one(position, shards_of):
        draws = jax.random.uniform(jax.random.fold_in(jax.random.fold_in(own_key, 6), position), (shards_of,), jnp.float32, least / len(split), largest / len(split))
        return jnp.repeat(jnp.exp(draws), shape[position] // shards_of).reshape((-1,) + (1,) * (len(shape) - position - 1))

    loudness = one(*split[0])
    for cut in split[1:]:
        loudness = loudness * one(*cut)
    return loudness


def centred(rng, shape, spread, most, pieces=(), dtype=jnp.bfloat16):
    factor_of = block_levels(rng, shape, pieces, -0.22, 0.18) if pieces else 1.0
    result = jax.random.normal(rng, shape, jnp.float32) * spread * factor_of
    return jnp.minimum(jnp.maximum(result, -most), most).astype(dtype)


def setup_inputs(seed: int = 0) -> dict:
    key_of = jax.random.split(jax.random.key(seed), 5)
    interior = centred(key_of[0], (NI, NB), (RI_DEV // 4) ** -0.5, 0.375, ((0, 16), (1, 8)))
    tile_mask = plant((jax.random.randint(key_of[1], (NI // 64, NB // 64), 0, 4) < 3).astype(jnp.int32), jax.random.fold_in(key_of[1], 1), 0, 1)
    owner = jax.random.randint(key_of[2], (STEPS,), 0, NB // PW).astype(jnp.int32)
    stiffness = centred(key_of[3], (STEPS, PW, NB), 0.5, 4.0, ((1, 16), (2, 8)), jnp.float32)
    return {"interior": interior, "tile_mask": tile_mask, "owner": owner, "stiffness": stiffness}


def expand(interior, tile_mask):
    rows, cols = interior.shape
    tiled = interior.reshape(rows // 64, 64, cols // 64, 64) * tile_mask.astype(jnp.bfloat16)[:, None, :, None]
    return tiled.reshape(rows, cols)


def reference(interior, tile_mask, owner, stiffness):
    masked = expand(interior, tile_mask)
    blocks = masked.reshape(N_WIDE, RI_DEV, NB)
    results = []
    for step_index in range(STEPS):
        first_col = (owner[step_index] * PW).astype(jnp.int32)
        panel_cols = lax.dynamic_slice_in_dim(masked, first_col, PW, 1)
        panel_blocks = panel_cols.reshape(N_WIDE, RI_DEV, PW)

        def add_block(total, pair):
            w_block, p_block = pair
            term = jnp.dot(p_block.T, w_block, preferred_element_type=jnp.float32)
            return total + term, None

        total, _ = lax.scan(add_block, jnp.zeros((PW, NB), jnp.float32), (blocks, panel_blocks))
        results.append(stiffness[step_index] - total)
    return jnp.stack(results)
```

```python
import functools

import jax
import jax.numpy as jnp
from jax import lax
from jax.experimental import pallas as pl
from jax.experimental.pallas import tpu as pltpu
from jax.sharding import PartitionSpec as P

PW = 512
STEPS = 2
MESH = pl.DeviceIdType.MESH
CHUNKS = 8
LAG = 4
HALF = 4096
DEPTH = 1024
GROUPS = ((0, 1280, (768, 512)), (1280, 1280, (768, 512)), (2560, 1536, (768, 768)))
THIRDS = ((0, 384), (384, 384), (768, 256))
TILE = 256


def pick_kernel(owner_ref, w_ref, mask_ref, out_ref):
    step, part = pl.program_id(0), pl.program_id(1)
    own = owner_ref[step]
    held = own // 16 == lax.axis_index("narrow")
    first_tile = (own % 16) * 8
    tile = lax.broadcasted_iota(jnp.int32, (128, PW), 0)
    column = lax.broadcasted_iota(jnp.int32, (128, PW), 1)
    wanted = jnp.where(held, first_tile, -1000) + column // 64
    spread = jnp.where(tile == wanted, 1.0, 0.0).astype(jnp.bfloat16)
    rows = mask_ref[pl.ds(pl.multiple_of(part * 8, 8), 8), :].astype(jnp.float32).astype(jnp.bfloat16)
    mask = jnp.dot(rows, spread, preferred_element_type=jnp.float32).astype(jnp.bfloat16)
    masked = jnp.concatenate([w_ref[64 * i : 64 * i + 64, :] * mask[i : i + 1, :] for i in range(8)], axis=0)
    place = lax.broadcasted_iota(jnp.int32, (PW, PW), 0)
    source = lax.broadcasted_iota(jnp.int32, (PW, PW), 1)
    u, v, x = (place // 64) % 2, (place // 32) % 2, (place // 16) % 2
    y = 2 * u + (u + v) % 2
    origin = y * 128 + x * 64 + ((place // 8) % 2) * 32 + (place // 128) * 8 + place % 8
    order = jnp.where(origin == source, 1.0, 0.0).astype(jnp.bfloat16)
    turned = lax.dot_general(order, masked, (((1,), (1,)), ((), ())), preferred_element_type=jnp.float32)
    out_ref[...] = turned.astype(jnp.bfloat16).reshape(4, 8, 16, PW)


def pick(owner, interior, tile_mask):
    return pl.pallas_call(
        pick_kernel,
        out_shape=jax.ShapeDtypeStruct((CHUNKS, 8, 16, DEPTH), jnp.bfloat16),
        grid_spec=pltpu.PrefetchScalarGridSpec(
            num_scalar_prefetch=1,
            grid=(STEPS, 2),
            in_specs=[
                pl.BlockSpec((PW, PW), lambda s, k, owner: (k, owner[s] % 16)),
                pl.BlockSpec((16, 128), lambda s, k, owner: (0, 0)),
            ],
            out_specs=pl.BlockSpec((4, 8, 16, PW), lambda s, k, owner: (s, 0, 0, k)),
        ),
    )(owner, interior, tile_mask)


def coded(values):
    most = jnp.maximum(jnp.max(jnp.abs(values), axis=0, keepdims=True), 1e-30)
    codes = jnp.round(values * (32767.0 / most)).astype(jnp.int32).astype(jnp.int16)
    return codes, most * (1.0 / 32767.0)


def main_kernel(
    w_hbm, mask_ref, cand, stiff_hbm, out_ref,
    b, a, r1, r2, mask2, keep, snd1, rcv1, snd2, rcv2, snd3, rcv3, snd4, rcv4, scs, scr,
    bc_s, bc_r, ac_s, ac_r, rd_s, rd_r, rs_s, rs_r, o_s, o_r, bl_s, br_s, br_r, m_s, m_r, st_s,
):
    w, n = lax.axis_index("wide"), lax.axis_index("narrow")
    core, x, y = w % 2, (w // 2) % 2, w // 4
    z, h = n // 2, n % 2
    u = y // 2
    v = (u + y % 2) % 2

    def at(y, x, core):
        return ((y * 2 + x) * 2 + core, n)

    twin = at(y, x, 1 - core)
    dims = {"v": (v, at(y + 1 - 2 * (y % 2), x, core)), "u": (u, at(3 - y, x, core)), "x": (x, at(y, 1 - x, core))}
    orders = ("vux", "uxv", "xvu")
    za, zb, hh = (w, (z + 1 - 2 * (z % 2)) * 2 + h), (w, (3 - z) * 2 + h), (w, z * 2 + 1 - h)
    routes = ((za, zb, hh), (zb, hh, za), (hh, za, zb))

    def remote(src, dst, s, r, device):
        return pltpu.make_async_remote_copy(
            src_ref=src, dst_ref=dst, send_sem=s, recv_sem=r, device_id=device, device_id_type=MESH
        )

    barrier = pltpu.get_barrier_semaphore()
    peers = (twin, dims["v"][1], dims["u"][1], dims["x"][1], za, zb, hh)
    for peer in peers:
        pl.semaphore_signal(barrier, inc=1, device_id=peer, device_id_type=MESH)

    def local_b(i):
        first = pl.multiple_of(core * HALF + i * 1024, 1024)
        return pltpu.make_async_copy(
            w_hbm.at[:, pl.ds(first, 1024)],
            b.at[pl.ds(0, DEPTH), pl.ds(pl.multiple_of(i * 1024, 1024), 1024)],
            bl_s.at[i],
        )

    def remote_b(i):
        first = pl.multiple_of((1 - core) * HALF + i * 1024, 1024)
        return remote(
            w_hbm.at[:, pl.ds(first, 1024)],
            b.at[pl.ds(DEPTH, DEPTH), pl.ds(pl.multiple_of(i * 1024, 1024), 1024)],
            br_s.at[i], br_r.at[i], twin,
        )

    mask_copy = remote(mask_ref, mask2, m_s.at[0], m_r.at[0], twin)
    stiff_copy = pltpu.make_async_copy(stiff_hbm, out_ref, st_s.at[0])

    def spread_copy(stage, third, t):
        first, width = THIRDS[third]
        cols = pl.ds(first, width)
        src = (cand, r1, r2)[stage]
        dst = (r1, r2, a)[stage]
        return remote(
            src.at[t, :, :, cols], dst.at[t, :, :, cols],
            bc_s.at[stage, third, t], bc_r.at[stage, third, t], routes[third][stage],
        )

    def twin_a(t):
        return remote(
            a.at[t, :, :, pl.ds(0, DEPTH)], a.at[t, :, :, pl.ds(DEPTH, DEPTH)], ac_s.at[t], ac_r.at[t], twin
        )

    def sum_copy(stage, g, t):
        src = (snd1, snd2, snd3)[stage][g]
        dst = (rcv1, rcv2, rcv3)[stage][g]
        peer = dims[orders[g][stage]][1]
        return (
            remote(src.at[t], dst.at[t], rd_s.at[stage, g, t], rd_r.at[stage, g, t], peer),
            remote(
                scs[g].at[stage, t], scr[g].at[stage, t], rs_s.at[stage, g, t], rs_r.at[stage, g, t], peer
            ),
        )

    def last_copy(g, t):
        return remote(snd4[g].at[t], rcv4[g].at[t], o_s.at[g, t], o_r.at[g, t], twin)

    for i in range(4):
        local_b(i).start()
    pl.semaphore_wait(barrier, len(peers))
    mask_copy.start()

    def spread_stage(stage, t):
        for third in range(3):
            first, width = THIRDS[third]
            cols = pl.ds(first, width)
            if stage > 0:
                spread_copy(stage - 1, third, t).wait_recv()
                if stage == 1:
                    r1[t, :, :, cols] = r1[t, :, :, cols] + cand[t, :, :, cols]
                if stage == 2:
                    r2[t, :, :, cols] = r2[t, :, :, cols] + r1[t, :, :, cols]
                if stage == 3:
                    a[t, :, :, cols] = a[t, :, :, cols] + r2[t, :, :, cols]
            if stage < 3:
                spread_copy(stage, third, t).start()
        if stage == 3:
            twin_a(t).start()

    def mask_slice(i):
        local_b(i).wait()
        remote_b(i).wait_recv()
        cols = pl.ds(pl.multiple_of(i * 1024, 1024), 1024)
        tile = lax.broadcasted_iota(jnp.int32, (128, 1024), 0)
        column = lax.broadcasted_iota(jnp.int32, (128, 1024), 1)
        wanted = core * 64 + i * 16 + column // 64
        spread = jnp.where(tile == wanted, 1.0, 0.0).astype(jnp.bfloat16)
        for half, ref in enumerate((mask_ref, mask2)):
            rows = ref[...].astype(jnp.float32).astype(jnp.bfloat16)
            mask = jnp.dot(rows, spread, preferred_element_type=jnp.float32).astype(jnp.bfloat16)
            for k in range(16):
                here = pl.ds(half * DEPTH + 64 * k, 64)
                b[here, cols] = b[here, cols] * mask[k : k + 1, :]

    def product(t):
        twin_a(t).wait_recv()
        for g, (first, width, tiles) in enumerate(GROUPS):
            names = orders[g]
            mine = dims[names[0]][0]

            def block(bit, second, third):
                bits = {names[0]: bit, names[1]: second, names[2]: third}
                return a[t, bits["u"] * 4 + bits["v"] * 2 + bits["x"]]

            lhs = jnp.concatenate(
                [block(bit, j, k) for bit in (1 - mine, mine) for j in (0, 1) for k in (0, 1)], axis=0
            )
            done = 0
            for size in tiles:
                here = pl.ds(done, size)
                both = jnp.dot(lhs, b[:, pl.ds(first + done, size)], preferred_element_type=jnp.float32)
                codes, scale = coded(both[:64])
                snd1[g][t, :, :, :, here] = codes.reshape(2, 2, 16, size)
                scs[g][0, t, :, here] = scale
                keep[g][t, :, :, :, here] = both[64:].reshape(2, 2, 16, size)
                done += size
            for copy in sum_copy(0, g, t):
                copy.start()

    def second(t):
        for g, (first, width, tiles) in enumerate(GROUPS):
            mine = dims[orders[g][1]][0]
            for copy in sum_copy(0, g, t):
                copy.wait_recv()

            def total(which, here, g=g):
                return keep[g][t, which, :, :, here] + rcv1[g][t, which, :, :, here].astype(jnp.int32).astype(
                    jnp.float32
                ) * scr[g][0, t, :, here].reshape(1, 1, TILE)

            def send(j, _, g=g, mine=mine):
                here = pl.ds(pl.multiple_of(j * TILE, TILE), TILE)
                codes, scale = coded(total(1 - mine, here).reshape(32, TILE))
                snd2[g][t, :, :, here] = codes.reshape(2, 16, TILE)
                scs[g][1, t, :, here] = scale
                return 0

            lax.fori_loop(0, width // TILE, send, 0)
            for copy in sum_copy(1, g, t):
                copy.start()

            def hold(j, _, g=g, mine=mine):
                here = pl.ds(pl.multiple_of(j * TILE, TILE), TILE)
                keep[g][t, mine, :, :, here] = total(mine, here)
                return 0

            lax.fori_loop(0, width // TILE, hold, 0)

    def third(t):
        for g, (first, width, tiles) in enumerate(GROUPS):
            mine2, mine3 = dims[orders[g][1]][0], dims[orders[g][2]][0]
            for copy in sum_copy(1, g, t):
                copy.wait_recv()

            def total(which, here, g=g):
                return keep[g][t, mine2, which, :, here] + rcv2[g][t, which, :, here].astype(jnp.int32).astype(
                    jnp.float32
                ) * scr[g][1, t, :, here]

            def send(j, _, g=g, mine3=mine3):
                here = pl.ds(pl.multiple_of(j * TILE, TILE), TILE)
                codes, scale = coded(total(1 - mine3, here))
                snd3[g][t, :, here] = codes
                scs[g][2, t, :, here] = scale
                return 0

            lax.fori_loop(0, width // TILE, send, 0)
            for copy in sum_copy(2, g, t):
                copy.start()

            def hold(j, _, g=g, mine2=mine2, mine3=mine3):
                here = pl.ds(pl.multiple_of(j * TILE, TILE), TILE)
                keep[g][t, mine2, mine3, :, here] = total(mine3, here)
                return 0

            lax.fori_loop(0, width // TILE, hold, 0)

    def fourth(t):
        step, rows = t // 4, pl.ds(pl.multiple_of((t % 4) * 8, 8), 8)
        for g, (first, width, tiles) in enumerate(GROUPS):
            mine2, mine3 = dims[orders[g][1]][0], dims[orders[g][2]][0]
            for copy in sum_copy(2, g, t):
                copy.wait_recv()

            def finish(j, _, g=g, first=first, mine2=mine2, mine3=mine3):
                here = pl.ds(pl.multiple_of(j * TILE, TILE), TILE)
                got = rcv3[g][t, :, here].astype(jnp.int32).astype(jnp.float32) * scr[g][2, t, :, here]
                total = keep[g][t, mine2, mine3, :, here] + got
                low, high = total[:8], total[8:]
                snd4[g][t, :, here] = jnp.where(core == 0, high, low)
                there = pl.ds(pl.multiple_of(core * HALF + first + j * TILE, TILE), TILE)
                out_ref[step, rows, there] = out_ref[step, rows, there] - jnp.where(core == 0, low, high)
                return 0

            lax.fori_loop(0, width // TILE, finish, 0)
            last_copy(g, t).start()

    def fifth(t):
        step, rows = t // 4, pl.ds(pl.multiple_of((t % 4) * 8, 8), 8)
        for g, (first, width, tiles) in enumerate(GROUPS):
            last_copy(g, t).wait_recv()
            there = pl.ds(pl.multiple_of((1 - core) * HALF + first, TILE), width)
            out_ref[step, rows, there] = out_ref[step, rows, there] - rcv4[g][t]

    def turn(i, _):
        def during(lag, body):
            @pl.when((i >= lag) & (i < lag + CHUNKS))
            def _():
                body(i - lag)

        during(0, lambda t: spread_stage(0, t))

        @pl.when(i == 0)
        def _():
            for j in range(4):
                remote_b(j).start()
            stiff_copy.start()
            mask_copy.wait_recv()

        during(1, lambda t: spread_stage(1, t))
        during(2, lambda t: spread_stage(2, t))
        during(3, lambda t: spread_stage(3, t))

        @pl.when(i < 4)
        def _():
            mask_slice(i)

        @pl.when(i == LAG + 3)
        def _():
            stiff_copy.wait()

        during(LAG, product)
        during(LAG + 1, second)
        during(LAG + 2, third)
        during(LAG + 3, fourth)
        during(LAG + 4, fifth)
        return 0

    lax.fori_loop(0, CHUNKS + LAG + 4, turn, 0)

    mask_copy.wait_send()
    for i in range(4):
        remote_b(i).wait_send()

    def drain(t, _):
        for stage in range(3):
            for third_ in range(3):
                spread_copy(stage, third_, t).wait_send()
            for g in range(3):
                for copy in sum_copy(stage, g, t):
                    copy.wait_send()
        twin_a(t).wait_send()
        for g in range(3):
            last_copy(g, t).wait_send()
        return 0

    lax.fori_loop(0, CHUNKS, drain, 0)


def shards(interior, tile_mask, owner, stiffness):
    cand = pick(owner, interior, tile_mask)
    widths = [width for _, width, _ in GROUPS]

    def each(dtype, *lead):
        return tuple(pltpu.VMEM((*lead, width), dtype) for width in widths)

    f32, i16, bf16 = jnp.float32, jnp.int16, jnp.bfloat16
    dma = pltpu.SemaphoreType.DMA
    return pl.pallas_call(
        main_kernel,
        out_shape=jax.ShapeDtypeStruct(stiffness.shape, f32),
        in_specs=[
            pl.BlockSpec(memory_space=pl.ANY),
            pl.BlockSpec(memory_space=pltpu.VMEM),
            pl.BlockSpec(memory_space=pltpu.VMEM),
            pl.BlockSpec(memory_space=pl.ANY),
        ],
        out_specs=pl.BlockSpec(memory_space=pltpu.VMEM),
        scratch_shapes=[
            pltpu.VMEM((2 * DEPTH, HALF), bf16),
            pltpu.VMEM((CHUNKS, 8, 16, 2 * DEPTH), bf16),
            pltpu.VMEM((CHUNKS, 8, 16, DEPTH), bf16),
            pltpu.VMEM((CHUNKS, 8, 16, DEPTH), bf16),
            pltpu.VMEM((16, 128), jnp.int32),
            each(f32, CHUNKS, 2, 2, 16),
            each(i16, CHUNKS, 2, 2, 16),
            each(i16, CHUNKS, 2, 2, 16),
            each(i16, CHUNKS, 2, 16),
            each(i16, CHUNKS, 2, 16),
            each(i16, CHUNKS, 16),
            each(i16, CHUNKS, 16),
            each(f32, CHUNKS, 8),
            each(f32, CHUNKS, 8),
            each(f32, 3, CHUNKS, 1),
            each(f32, 3, CHUNKS, 1),
            dma((3, 3, CHUNKS)), dma((3, 3, CHUNKS)),
            dma((CHUNKS,)), dma((CHUNKS,)),
            dma((3, 3, CHUNKS)), dma((3, 3, CHUNKS)),
            dma((3, 3, CHUNKS)), dma((3, 3, CHUNKS)),
            dma((3, CHUNKS)), dma((3, CHUNKS)),
            dma((4,)), dma((4,)), dma((4,)),
            dma((1,)), dma((1,)), dma((1,)),
        ],
        compiler_params=pltpu.CompilerParams(
            collective_id=0, has_side_effects=True, vmem_limit_bytes=62 * 1024 * 1024
        ),
    )(interior, tile_mask, cand, stiffness)


def solution(mesh):
    placed = (P("wide", "narrow"), P("wide", "narrow"), P(), P(None, "wide", "narrow"))
    return jax.shard_map(
        shards, mesh=mesh, in_specs=placed, out_specs=P(None, "wide", "narrow"), check_vma=False
    )
```

```python
import functools

import jax
import jax.numpy as jnp
from jax import lax
from jax.experimental import pallas as pl
from jax.experimental.pallas import tpu as pltpu
from jax.sharding import PartitionSpec as P

PW = 512
STEPS = 2
MESH = pl.DeviceIdType.MESH
CHUNKS = 8
SLOTS = 4
LAG = 4
HALF = 4096
DEPTH = 1024
GROUPS = ((0, 1792, (768, 512, 512)), (1792, 1536, (768, 768)), (3328, 768, (768,)))
TILE = 256


def pick_kernel(owner_ref, w_ref, mask_ref, out_ref, order):
    step, part = pl.program_id(0), pl.program_id(1)
    own = owner_ref[step]
    held = own // 16 == lax.axis_index("narrow")
    first_tile = (own % 16) * 8
    tile = lax.broadcasted_iota(jnp.int32, (128, PW), 0)
    column = lax.broadcasted_iota(jnp.int32, (128, PW), 1)
    wanted = jnp.where(held, first_tile, -1000) + column // 64
    spread = jnp.where(tile == wanted, 1.0, 0.0).astype(jnp.bfloat16)
    rows = mask_ref[pl.ds(pl.multiple_of(part * 8, 8), 8), :].astype(jnp.float32).astype(jnp.bfloat16)
    mask = jnp.dot(rows, spread, preferred_element_type=jnp.float32)
    pieces = []
    for i in range(8):
        factor = jnp.broadcast_to(mask[i : i + 1, :], (16, PW)).astype(jnp.bfloat16)
        pieces += [w_ref[k : k + 16, :] * factor for k in range(64 * i, 64 * i + 64, 16)]
    masked = jnp.concatenate(pieces, axis=0)
    @pl.when((step == 0) & (part == 0))
    def _():
        place = lax.broadcasted_iota(jnp.int32, (PW, 1), 0)
        source = lax.broadcasted_iota(jnp.int32, (PW, PW), 1)
        u, v, x = (place // 64) % 2, (place // 32) % 2, (place // 16) % 2
        y = 2 * u + (u + v) % 2
        origin = y * 128 + x * 64 + ((place // 8) % 2) * 32 + (place // 128) * 8 + place % 8
        order[...] = jnp.where(origin == source, 1.0, 0.0).astype(jnp.bfloat16)

    turned = lax.dot_general(order[...], masked, (((1,), (1,)), ((), ())), preferred_element_type=jnp.float32)
    out_ref[...] = turned.astype(jnp.bfloat16).reshape(4, 8, 16, PW)


def pick(owner, interior, tile_mask):
    return pl.pallas_call(
        pick_kernel,
        out_shape=jax.ShapeDtypeStruct((CHUNKS, 8, 16, DEPTH), jnp.bfloat16),
        grid_spec=pltpu.PrefetchScalarGridSpec(
            num_scalar_prefetch=1,
            grid=(STEPS, 2),
            in_specs=[
                pl.BlockSpec((PW, PW), lambda s, k, owner: (k, owner[s] % 16)),
                pl.BlockSpec((16, 128), lambda s, k, owner: (0, 0)),
            ],
            out_specs=pl.BlockSpec((4, 8, 16, PW), lambda s, k, owner: (s, 0, 0, k)),
            scratch_shapes=[pltpu.VMEM((PW, PW), jnp.bfloat16)],
        ),
    )(owner, interior, tile_mask)


def coded(values):
    most = jnp.maximum(jnp.max(jnp.abs(values), axis=0, keepdims=True), 1e-30)
    codes = jnp.round(values * (32767.0 / most)).astype(jnp.int32).astype(jnp.int16)
    return codes, most * (1.0 / 32767.0)


def main_kernel(
    w_hbm, mask_ref, cand, stiff_hbm, out_hbm,
    out_ref, mine_c, b, a, r1, s1, r2, mask2, keep, snd1, rcv1, snd2, rcv2, snd3, rcv3, snd4, rcv4, scs, scr,
    c1_s, c1_r, c2_s, c2_r, c3_s, c3_r, ac_s, ac_r, rd_s, rd_r, rs_s, rs_r, o_s, o_r, bl_s, br_s, br_r, m_s, m_r, st_s, mc_s, w_s,
):
    w, n = lax.axis_index("wide"), lax.axis_index("narrow")
    core, x, y = w % 2, (w // 2) % 2, w // 4
    z, h = n // 2, n % 2
    u = y // 2
    v = (u + y % 2) % 2

    def at(y, x, core):
        return ((y * 2 + x) * 2 + core, n)

    twin = at(y, x, 1 - core)
    dims = {"v": (v, at(y + 1 - 2 * (y % 2), x, core)), "u": (u, at(3 - y, x, core)), "x": (x, at(y, 1 - x, core))}
    orders = ("vux", "uxv", "xvu")
    others = [(z + d) % 4 for d in (1, 2, 3)]
    ring = [(w, other * 2 + h) for other in others]
    across = (w, z * 2 + 1 - h)

    def remote(src, dst, s, r, device):
        return pltpu.make_async_remote_copy(
            src_ref=src, dst_ref=dst, send_sem=s, recv_sem=r, device_id=device, device_id_type=MESH
        )

    barrier = pltpu.get_barrier_semaphore()
    peers = (twin, dims["v"][1], dims["u"][1], dims["x"][1], *ring, across)
    for peer in peers:
        pl.semaphore_signal(barrier, inc=1, device_id=peer, device_id_type=MESH)

    def local_b(i):
        first = pl.multiple_of(core * HALF + i * 1024, 1024)
        return pltpu.make_async_copy(
            w_hbm.at[:, pl.ds(first, 1024)],
            b.at[pl.ds(0, DEPTH), pl.ds(pl.multiple_of(i * 1024, 1024), 1024)],
            bl_s.at[i],
        )

    def remote_b(i):
        first = pl.multiple_of((1 - core) * HALF + i * 1024, 1024)
        return remote(
            w_hbm.at[:, pl.ds(first, 1024)],
            b.at[pl.ds(DEPTH, DEPTH), pl.ds(pl.multiple_of(i * 1024, 1024), 1024)],
            br_s.at[i], br_r.at[i], twin,
        )

    mask_copy = remote(mask_ref, mask2, m_s.at[0], m_r.at[0], twin)
    stiff_copy = pltpu.make_async_copy(stiff_hbm, out_ref, st_s.at[0])
    mine_copy = pltpu.make_async_copy(cand.at[:, pl.ds(2 * z, 2)], mine_c, mc_s.at[0])

    def out_copy(t):
        rows = pl.ds(pl.multiple_of((t % 4) * 8, 8), 8)
        return pltpu.make_async_copy(out_ref.at[t // 4, rows], out_hbm.at[t // 4, rows], w_s.at[t])


    def quarter(z):
        return pl.ds(2 * z, 2)

    def scatter(d, t):
        return remote(cand.at[t, quarter(others[d])], r1.at[t, d], c1_s.at[d, t % SLOTS], c1_r.at[d, t % SLOTS], ring[d])

    def cross(t):
        return remote(s1.at[t], r2.at[t], c2_s.at[t % SLOTS], c2_r.at[t % SLOTS], across)

    def gather(d, t):
        piece = a.at[t, 0, quarter(z)]
        return remote(piece, piece, c3_s.at[d, t % SLOTS], c3_r.at[d, t % SLOTS], ring[d])

    def twin_a(t):
        return remote(a.at[t, 0], a.at[t, 1], ac_s.at[t % SLOTS], ac_r.at[t % SLOTS], twin)

    def sum_copy(stage, g, t):
        src = (snd1, snd2, snd3)[stage][g]
        dst = (rcv1, rcv2, rcv3)[stage][g]
        peer = dims[orders[g][stage]][1]
        slot = t % SLOTS
        return (
            remote(src.at[t], dst.at[t], rd_s.at[stage, g, slot], rd_r.at[stage, g, slot], peer),
            remote(scs[g].at[stage, t], scr[g].at[stage, t], rs_s.at[stage, g, slot], rs_r.at[stage, g, slot], peer),
        )

    def last_copy(g, t):
        return remote(snd4[g].at[t], rcv4[g].at[t], o_s.at[g, t % SLOTS], o_r.at[g, t % SLOTS], twin)

    mine_copy.start()
    for i in range(4):
        local_b(i).start()
    pl.semaphore_wait(barrier, len(peers))
    mask_copy.start()

    def launch(t, copies):
        @pl.when(t >= SLOTS)
        def _():
            for copy in copies(t - SLOTS):
                copy.wait_send()

        for copy in copies(t):
            copy.start()

    def scatters(t):
        return [scatter(d, t) for d in range(3)]

    def gathers(t):
        return [gather(d, t) for d in range(3)]

    def spread_0(t):
        launch(t, scatters)

    def spread_1(t):
        for copy in scatters(t):
            copy.wait_recv()
        s1[t] = (mine_c[t] + r1[t, 0]) + (r1[t, 1] + r1[t, 2])
        launch(t, lambda t: [cross(t)])

    def spread_2(t):
        cross(t).wait_recv()
        a[t, 0, quarter(z)] = s1[t] + r2[t]
        launch(t, gathers)

    def spread_3(t):
        for copy in gathers(t):
            copy.wait_recv()
        launch(t, lambda t: [twin_a(t)])

    def mask_slice(half, ref, i):
        cols = pl.ds(pl.multiple_of(i * 1024, 1024), 1024)
        tile = lax.broadcasted_iota(jnp.int32, (128, 1024), 0)
        column = lax.broadcasted_iota(jnp.int32, (1, 1024), 1)
        wanted = core * 64 + i * 16 + column // 64
        spread = jnp.where(tile == wanted, 1.0, 0.0).astype(jnp.bfloat16)
        rows = ref[...].astype(jnp.float32).astype(jnp.bfloat16)
        mask = jnp.dot(rows, spread, preferred_element_type=jnp.float32)
        for k in range(16):
            factor = jnp.broadcast_to(mask[k : k + 1, :], (16, 1024)).astype(jnp.bfloat16)
            for row in range(half * DEPTH + 64 * k, half * DEPTH + 64 * k + 64, 16):
                b[row : row + 16, cols] = b[row : row + 16, cols] * factor

    def product(t):
        twin_a(t).wait_recv()
        for g, (first, width, tiles) in enumerate(GROUPS):
            if g == 1:

                @pl.when(t == 0)
                def _():
                    for j in (2, 3):
                        remote_b(j).wait_recv()
                        mask_slice(1, mask2, j)

            names = orders[g]
            mine = dims[names[0]][0]

            def block(bit, second, third):
                bits = {names[0]: bit, names[1]: second, names[2]: third}
                index = bits["u"] * 4 + bits["v"] * 2 + bits["x"]
                return jnp.concatenate([a[t, 0, index], a[t, 1, index]], axis=1)

            lhs = jnp.concatenate(
                [block(bit, j, k) for bit in (1 - mine, mine) for j in (0, 1) for k in (0, 1)], axis=0
            )
            done = 0
            for size in tiles:
                here = pl.ds(done, size)
                both = jnp.dot(lhs, b[:, pl.ds(first + done, size)], preferred_element_type=jnp.float32)
                codes, scale = coded(both[:64])
                snd1[g][t, :, :, :, here] = codes.reshape(2, 2, 16, size)
                scs[g][0, t, :, here] = scale
                keep[g][t, :, :, :, here] = both[64:].reshape(2, 2, 16, size)
                done += size
            launch(t, functools.partial(sum_copy, 0, g))

    def second(t):
        for g, (first, width, tiles) in enumerate(GROUPS):
            mine = dims[orders[g][1]][0]
            for copy in sum_copy(0, g, t):
                copy.wait_recv()

            def total(which, here, g=g):
                return keep[g][t, which, :, :, here] + rcv1[g][t, which, :, :, here].astype(jnp.int32).astype(
                    jnp.float32
                ) * scr[g][0, t, :, here].reshape(1, 1, TILE)

            def send(j, _, g=g, mine=mine):
                here = pl.ds(pl.multiple_of(j * TILE, TILE), TILE)
                codes, scale = coded(total(1 - mine, here).reshape(32, TILE))
                snd2[g][t, :, :, here] = codes.reshape(2, 16, TILE)
                scs[g][1, t, :, here] = scale
                return 0

            lax.fori_loop(0, width // TILE, send, 0)
            launch(t, functools.partial(sum_copy, 1, g))

            def hold(j, _, g=g, mine=mine):
                here = pl.ds(pl.multiple_of(j * TILE, TILE), TILE)
                keep[g][t, mine, :, :, here] = total(mine, here)
                return 0

            lax.fori_loop(0, width // TILE, hold, 0)

    def third(t):
        for g, (first, width, tiles) in enumerate(GROUPS):
            mine2, mine3 = dims[orders[g][1]][0], dims[orders[g][2]][0]
            for copy in sum_copy(1, g, t):
                copy.wait_recv()

            def total(which, here, g=g):
                return keep[g][t, mine2, which, :, here] + rcv2[g][t, which, :, here].astype(jnp.int32).astype(
                    jnp.float32
                ) * scr[g][1, t, :, here]

            def send(j, _, g=g, mine3=mine3):
                here = pl.ds(pl.multiple_of(j * TILE, TILE), TILE)
                codes, scale = coded(total(1 - mine3, here))
                snd3[g][t, :, here] = codes
                scs[g][2, t, :, here] = scale
                return 0

            lax.fori_loop(0, width // TILE, send, 0)
            launch(t, functools.partial(sum_copy, 2, g))

            def hold(j, _, g=g, mine2=mine2, mine3=mine3):
                here = pl.ds(pl.multiple_of(j * TILE, TILE), TILE)
                keep[g][t, mine2, mine3, :, here] = total(mine3, here)
                return 0

            lax.fori_loop(0, width // TILE, hold, 0)

    def fourth(t):
        step, rows = t // 4, pl.ds(pl.multiple_of((t % 4) * 8, 8), 8)
        for g, (first, width, tiles) in enumerate(GROUPS):
            mine2, mine3 = dims[orders[g][1]][0], dims[orders[g][2]][0]
            for copy in sum_copy(2, g, t):
                copy.wait_recv()

            def finish(j, _, g=g, first=first, mine2=mine2, mine3=mine3):
                here = pl.ds(pl.multiple_of(j * TILE, TILE), TILE)
                got = rcv3[g][t, :, here].astype(jnp.int32).astype(jnp.float32) * scr[g][2, t, :, here]
                total = keep[g][t, mine2, mine3, :, here] + got
                low, high = total[:8], total[8:]
                snd4[g][t, :, here] = jnp.where(core == 0, high, low)
                there = pl.ds(pl.multiple_of(core * HALF + first + j * TILE, TILE), TILE)
                out_ref[step, rows, there] = out_ref[step, rows, there] - jnp.where(core == 0, low, high)
                return 0

            lax.fori_loop(0, width // TILE, finish, 0)
            launch(t, lambda t, g=g: [last_copy(g, t)])

    def fifth(t):
        step, rows = t // 4, pl.ds(pl.multiple_of((t % 4) * 8, 8), 8)
        for g, (first, width, tiles) in enumerate(GROUPS):
            last_copy(g, t).wait_recv()
            there = pl.ds(pl.multiple_of((1 - core) * HALF + first, TILE), width)
            out_ref[step, rows, there] = out_ref[step, rows, there] - rcv4[g][t]
        out_copy(t).start()

    def turn(i, _):
        def during(lag, body):
            @pl.when((i >= lag) & (i < lag + CHUNKS))
            def _():
                body(i - lag)

        @pl.when(i < LAG)
        def _():
            during(3, spread_3)
            during(2, spread_2)
            during(1, spread_1)
            during(0, spread_0)

        @pl.when(i == 0)
        def _():
            for j in range(4):
                remote_b(j).start()
            stiff_copy.start()
            mine_copy.wait()
            mask_copy.wait_recv()

        @pl.when(i < 2)
        def _():
            for j in range(2):
                local_b(2 * i + j).wait()
                mask_slice(0, mask_ref, 2 * i + j)

        @pl.when(i == 3)
        def _():
            for j in range(2):
                remote_b(j).wait_recv()
                mask_slice(1, mask2, j)

        during(LAG, product)

        @pl.when(i >= LAG)
        def _():
            during(0, spread_0)
            during(1, spread_1)
            during(2, spread_2)
            during(3, spread_3)

        @pl.when(i == LAG + 3)
        def _():
            stiff_copy.wait()

        during(LAG + 1, second)
        during(LAG + 2, third)
        during(LAG + 3, fourth)
        during(LAG + 4, fifth)
        return 0

    lax.fori_loop(0, CHUNKS + LAG + 4, turn, 0)

    mask_copy.wait_send()
    for i in range(4):
        remote_b(i).wait_send()

    def written(t, _):
        out_copy(t).wait()
        return 0

    lax.fori_loop(0, CHUNKS, written, 0)

    def drain(t, _):
        for stage in range(3):
            for g in range(3):
                for copy in sum_copy(stage, g, t):
                    copy.wait_send()
        for d in range(3):
            scatter(d, t).wait_send()
            gather(d, t).wait_send()
        cross(t).wait_send()
        twin_a(t).wait_send()
        for g in range(3):
            last_copy(g, t).wait_send()
        return 0

    lax.fori_loop(CHUNKS - SLOTS, CHUNKS, drain, 0)


def shards(interior, tile_mask, owner, stiffness):
    cand = pick(owner, interior, tile_mask)
    widths = [width for _, width, _ in GROUPS]

    def each(dtype, *lead):
        return tuple(pltpu.VMEM((*lead, width), dtype) for width in widths)

    f32, i16, bf16 = jnp.float32, jnp.int16, jnp.bfloat16
    dma = pltpu.SemaphoreType.DMA
    return pl.pallas_call(
        main_kernel,
        out_shape=jax.ShapeDtypeStruct(stiffness.shape, f32),
        in_specs=[
            pl.BlockSpec(memory_space=pl.ANY),
            pl.BlockSpec(memory_space=pltpu.VMEM),
            pl.BlockSpec(memory_space=pl.ANY),
            pl.BlockSpec(memory_space=pl.ANY),
        ],
        out_specs=pl.BlockSpec(memory_space=pl.ANY),
        scratch_shapes=[
            pltpu.VMEM((STEPS, 32, 2 * HALF), f32),
            pltpu.VMEM((CHUNKS, 2, 16, DEPTH), bf16),
            pltpu.VMEM((2 * DEPTH, HALF), bf16),
            pltpu.VMEM((CHUNKS, 2, 8, 16, DEPTH), bf16),
            pltpu.VMEM((CHUNKS, 3, 2, 16, DEPTH), bf16),
            pltpu.VMEM((CHUNKS, 2, 16, DEPTH), bf16),
            pltpu.VMEM((CHUNKS, 2, 16, DEPTH), bf16),
            pltpu.VMEM((16, 128), jnp.int32),
            each(f32, CHUNKS, 2, 2, 16),
            each(i16, CHUNKS, 2, 2, 16),
            each(i16, CHUNKS, 2, 2, 16),
            each(i16, CHUNKS, 2, 16),
            each(i16, CHUNKS, 2, 16),
            each(i16, CHUNKS, 16),
            each(i16, CHUNKS, 16),
            each(f32, CHUNKS, 8),
            each(f32, CHUNKS, 8),
            each(f32, 3, CHUNKS, 1),
            each(f32, 3, CHUNKS, 1),
            dma((3, SLOTS)), dma((3, SLOTS)), dma((SLOTS,)), dma((SLOTS,)), dma((3, SLOTS)), dma((3, SLOTS)),
            dma((SLOTS,)), dma((SLOTS,)),
            dma((3, 3, SLOTS)), dma((3, 3, SLOTS)),
            dma((3, 3, SLOTS)), dma((3, 3, SLOTS)),
            dma((3, SLOTS)), dma((3, SLOTS)),
            dma((4,)), dma((4,)), dma((4,)),
            dma((1,)), dma((1,)), dma((1,)), dma((1,)), dma((CHUNKS,)),
        ],
        compiler_params=pltpu.CompilerParams(
            collective_id=0, has_side_effects=True, vmem_limit_bytes=62 * 1024 * 1024
        ),
    )(interior, tile_mask, cand, stiffness)


def solution(mesh):
    placed = (P("wide", "narrow"), P("wide", "narrow"), P(), P(None, "wide", "narrow"))
    return jax.shard_map(
        shards, mesh=mesh, in_specs=placed, out_specs=P(None, "wide", "narrow"), check_vma=False
    )
```

```python
import functools

import jax
import jax.numpy as jnp
from jax import lax
from jax.experimental import pallas as pl
from jax.experimental.pallas import tpu as pltpu
from jax.sharding import PartitionSpec as P

PW = 512
STEPS = 2
MESH = pl.DeviceIdType.MESH
CHUNKS = 8
SLOTS = 4
LAG = 4
HALF = 4096
DEPTH = 1024
GROUPS = ((0, 1792, (1024, 768)), (1792, 1408, (768, 640)), (3200, 896, (896,)))
TILES = (256, 128, 128)


def pick_kernel(owner_ref, w_hbm, mask_ref, out_hbm, order, blocks, turned, in_sem, out_sem):
    parts = [(step, part) for step in range(STEPS) for part in range(2)]

    def fetch(step, part):
        first = pl.multiple_of(owner_ref[step] % 16 * PW, PW)
        here = 2 * step + part
        return pltpu.make_async_copy(
            w_hbm.at[pl.ds(part * PW, PW), pl.ds(first, PW)], blocks.at[here], in_sem.at[here]
        )

    def leave(step, part):
        here = 2 * step + part
        return pltpu.make_async_copy(
            turned.at[here], out_hbm.at[pl.ds(4 * step, 4), :, :, pl.ds(part * PW, PW)], out_sem.at[here]
        )

    for step, part in parts:
        fetch(step, part).start()
    place = lax.broadcasted_iota(jnp.int32, (PW, 1), 0)
    source = lax.broadcasted_iota(jnp.int32, (PW, PW), 1)
    u, v, x = (place // 64) % 2, (place // 32) % 2, (place // 16) % 2
    y = 2 * u + (u + v) % 2
    origin = y * 128 + x * 64 + ((place // 8) % 2) * 32 + (place // 128) * 8 + place % 8
    order[...] = jnp.where(origin == source, 1.0, 0.0).astype(jnp.bfloat16)
    tile = lax.broadcasted_iota(jnp.int32, (128, PW), 0)
    column = lax.broadcasted_iota(jnp.int32, (1, PW), 1)
    rows = mask_ref[...].astype(jnp.float32).astype(jnp.bfloat16)
    for step in range(STEPS):
        own = owner_ref[step]
        held = own // 16 == lax.axis_index("narrow")
        wanted = jnp.where(held, (own % 16) * 8, -1000) + column // 64
        spread = jnp.where(tile == wanted, 1.0, 0.0).astype(jnp.bfloat16)
        mask = jnp.dot(rows, spread, preferred_element_type=jnp.float32)
        for part in range(2):
            here = 2 * step + part
            fetch(step, part).wait()
            pieces = []
            for i in range(8):
                row = 8 * part + i
                factor = jnp.broadcast_to(mask[row : row + 1, :], (16, PW)).astype(jnp.bfloat16)
                pieces += [blocks[here, k : k + 16, :] * factor for k in range(64 * i, 64 * i + 64, 16)]
            masked = jnp.concatenate(pieces, axis=0)
            product = lax.dot_general(
                order[...], masked, (((1,), (1,)), ((), ())), preferred_element_type=jnp.float32
            )
            turned[here] = product.astype(jnp.bfloat16).reshape(4, 8, 16, PW)
            leave(step, part).start()
    for step, part in parts:
        leave(step, part).wait()


def pick(owner, interior, tile_mask):
    return pl.pallas_call(
        pick_kernel,
        out_shape=jax.ShapeDtypeStruct((CHUNKS, 8, 16, DEPTH), jnp.bfloat16),
        in_specs=[
            pl.BlockSpec(memory_space=pltpu.SMEM),
            pl.BlockSpec(memory_space=pl.ANY),
            pl.BlockSpec(memory_space=pltpu.VMEM),
        ],
        out_specs=pl.BlockSpec(memory_space=pl.ANY),
        scratch_shapes=[
            pltpu.VMEM((PW, PW), jnp.bfloat16),
            pltpu.VMEM((4, PW, PW), jnp.bfloat16),
            pltpu.VMEM((4, 4, 8, 16, PW), jnp.bfloat16),
            pltpu.SemaphoreType.DMA((4,)),
            pltpu.SemaphoreType.DMA((4,)),
        ],
    )(owner, interior, tile_mask)


def hand_over_kernel(source, target, buffer, in_sem, out_sem):
    def move(t, inward):
        rows = pl.ds((t % 4) * 8, 8)
        if inward:
            return pltpu.make_async_copy(source.at[t // 4, rows], buffer.at[t], in_sem.at[t])
        return pltpu.make_async_copy(buffer.at[t], target.at[t // 4, rows], out_sem.at[t])

    for t in range(CHUNKS):
        move(t, True).start()
    for t in range(CHUNKS):
        move(t, True).wait()
        move(t, False).start()
    for t in range(CHUNKS):
        move(t, False).wait()


def hand_over(result):
    return pl.pallas_call(
        hand_over_kernel,
        out_shape=jax.ShapeDtypeStruct(result.shape, result.dtype),
        in_specs=[pl.BlockSpec(memory_space=pl.ANY)],
        out_specs=pl.BlockSpec(memory_space=pl.ANY),
        scratch_shapes=[
            pltpu.VMEM((CHUNKS, 8, 2 * HALF), jnp.float32),
            pltpu.SemaphoreType.DMA((CHUNKS,)),
            pltpu.SemaphoreType.DMA((CHUNKS,)),
        ],
    )(result)


def coded(values):
    most = jnp.maximum(jnp.max(jnp.abs(values), axis=0, keepdims=True), 1e-30)
    codes = jnp.round(values * (32767.0 / most)).astype(jnp.int32).astype(jnp.int16)
    return codes, most * (1.0 / 32767.0)


def main_kernel(
    w_hbm, mask_ref, cand, stiff_hbm, out_hbm,
    out_ref, mine_c, b, a, r1, s1, r2, mask2, keep, snd1, rcv1, snd2, rcv2, snd3, rcv3, snd4, rcv4, scs, scr,
    c1_s, c1_r, c2_s, c2_r, c3_s, c3_r, ac_s, ac_r, rd_s, rd_r, rs_s, rs_r, o_s, o_r, bl_s, br_s, br_r, m_s, m_r, st_s, mc_s, w_s,
):
    w, n = lax.axis_index("wide"), lax.axis_index("narrow")
    core, x, y = w % 2, (w // 2) % 2, w // 4
    z, h = n // 2, n % 2
    u = y // 2
    v = (u + y % 2) % 2

    def at(y, x, core):
        return ((y * 2 + x) * 2 + core, n)

    twin = at(y, x, 1 - core)
    dims = {"v": (v, at(y + 1 - 2 * (y % 2), x, core)), "u": (u, at(3 - y, x, core)), "x": (x, at(y, 1 - x, core))}
    orders = ("vux", "uxv", "xvu")
    others = [(z + d) % 4 for d in (1, 2, 3)]
    ring = [(w, other * 2 + h) for other in others]
    across = (w, z * 2 + 1 - h)

    def remote(src, dst, s, r, device):
        return pltpu.make_async_remote_copy(
            src_ref=src, dst_ref=dst, send_sem=s, recv_sem=r, device_id=device, device_id_type=MESH
        )

    barrier = pltpu.get_barrier_semaphore()
    peers = (twin, dims["v"][1], dims["u"][1], dims["x"][1], *ring, across)
    for peer in peers:
        pl.semaphore_signal(barrier, inc=1, device_id=peer, device_id_type=MESH)

    def local_b(i):
        first = pl.multiple_of(core * HALF + i * 1024, 1024)
        return pltpu.make_async_copy(
            w_hbm.at[:, pl.ds(first, 1024)],
            b.at[pl.ds(0, DEPTH), pl.ds(pl.multiple_of(i * 1024, 1024), 1024)],
            bl_s.at[i],
        )

    def remote_b(i):
        first = pl.multiple_of((1 - core) * HALF + i * 1024, 1024)
        return remote(
            w_hbm.at[:, pl.ds(first, 1024)],
            b.at[pl.ds(DEPTH, DEPTH), pl.ds(pl.multiple_of(i * 1024, 1024), 1024)],
            br_s.at[i], br_r.at[i], twin,
        )

    mask_copy = remote(mask_ref, mask2, m_s.at[0], m_r.at[0], twin)
    stiff_copy = pltpu.make_async_copy(stiff_hbm, out_ref, st_s.at[0])
    mine_copy = pltpu.make_async_copy(cand.at[:, pl.ds(2 * z, 2)], mine_c, mc_s.at[0])

    def out_copy(t):
        rows = pl.ds(pl.multiple_of((t % 4) * 8, 8), 8)
        return pltpu.make_async_copy(out_ref.at[t // 4, rows], out_hbm.at[t // 4, rows], w_s.at[t])


    def quarter(z):
        return pl.ds(2 * z, 2)

    def scatter(d, t):
        return remote(cand.at[t, quarter(others[d])], r1.at[t, d], c1_s.at[d, t % SLOTS], c1_r.at[d, t % SLOTS], ring[d])

    def cross(t):
        return remote(s1.at[t], r2.at[t], c2_s.at[t % SLOTS], c2_r.at[t % SLOTS], across)

    def gather(d, t):
        piece = a.at[t, 0, quarter(z)]
        return remote(piece, piece, c3_s.at[d, t % SLOTS], c3_r.at[d, t % SLOTS], ring[d])

    def twin_a(t):
        return remote(a.at[t, 0], a.at[t, 1], ac_s.at[t % SLOTS], ac_r.at[t % SLOTS], twin)

    def sum_copy(stage, g, t):
        src = (snd1, snd2, snd3)[stage][g]
        dst = (rcv1, rcv2, rcv3)[stage][g]
        peer = dims[orders[g][stage]][1]
        slot = t % SLOTS
        return (
            remote(src.at[t], dst.at[t], rd_s.at[stage, g, slot], rd_r.at[stage, g, slot], peer),
            remote(scs[g].at[stage, t], scr[g].at[stage, t], rs_s.at[stage, g, slot], rs_r.at[stage, g, slot], peer),
        )

    def last_copy(g, t):
        return remote(snd4[g].at[t], rcv4[g].at[t], o_s.at[g, t % SLOTS], o_r.at[g, t % SLOTS], twin)

    mine_copy.start()
    for i in range(4):
        local_b(i).start()
    pl.semaphore_wait(barrier, len(peers))
    mask_copy.start()

    def launch(t, copies):
        @pl.when(t >= SLOTS)
        def _():
            for copy in copies(t - SLOTS):
                copy.wait_send()

        for copy in copies(t):
            copy.start()

    def scatters(t):
        return [scatter(d, t) for d in range(3)]

    def gathers(t):
        return [gather(d, t) for d in range(3)]

    def spread_0(t):
        launch(t, scatters)

    def spread_1(t):
        for copy in scatters(t):
            copy.wait_recv()
        s1[t] = (mine_c[t] + r1[t, 0]) + (r1[t, 1] + r1[t, 2])
        launch(t, lambda t: [cross(t)])

    def spread_2(t):
        cross(t).wait_recv()
        a[t, 0, quarter(z)] = s1[t] + r2[t]
        launch(t, gathers)

    def spread_3(t):
        for copy in gathers(t):
            copy.wait_recv()
        launch(t, lambda t: [twin_a(t)])

    def mask_slice(half, ref, i):
        cols = pl.ds(pl.multiple_of(i * 1024, 1024), 1024)
        tile = lax.broadcasted_iota(jnp.int32, (128, 1024), 0)
        column = lax.broadcasted_iota(jnp.int32, (1, 1024), 1)
        wanted = core * 64 + i * 16 + column // 64
        spread = jnp.where(tile == wanted, 1.0, 0.0).astype(jnp.bfloat16)
        rows = ref[...].astype(jnp.float32).astype(jnp.bfloat16)
        mask = jnp.dot(rows, spread, preferred_element_type=jnp.float32)
        for k in range(16):
            factor = jnp.broadcast_to(mask[k : k + 1, :], (16, 1024)).astype(jnp.bfloat16)
            for row in range(half * DEPTH + 64 * k, half * DEPTH + 64 * k + 64, 16):
                b[row : row + 16, cols] = b[row : row + 16, cols] * factor

    def product(t):
        twin_a(t).wait_recv()
        for g, (first, width, tiles) in enumerate(GROUPS):
            if g == 1:

                @pl.when(t == 0)
                def _():
                    for j in (2, 3):
                        remote_b(j).wait_recv()
                        mask_slice(1, mask2, j)

            names = orders[g]
            mine = dims[names[0]][0]

            def block(bit, second, third):
                bits = {names[0]: bit, names[1]: second, names[2]: third}
                index = bits["u"] * 4 + bits["v"] * 2 + bits["x"]
                return jnp.concatenate([a[t, 0, index], a[t, 1, index]], axis=1)

            lhs = jnp.concatenate(
                [block(bit, j, k) for bit in (1 - mine, mine) for j in (0, 1) for k in (0, 1)], axis=0
            )
            done = 0
            for size in tiles:
                here = pl.ds(done, size)
                both = jnp.dot(lhs, b[:, pl.ds(first + done, size)], preferred_element_type=jnp.float32)
                codes, scale = coded(both[:64])
                snd1[g][t, :, :, :, here] = codes.reshape(2, 2, 16, size)
                scs[g][0, t, :, here] = scale
                keep[g][t, :, :, :, here] = both[64:].reshape(2, 2, 16, size)
                done += size
            launch(t, functools.partial(sum_copy, 0, g))

    def second(t):
        for g, (first, width, tiles) in enumerate(GROUPS):
            size = TILES[g]
            mine = dims[orders[g][1]][0]
            for copy in sum_copy(0, g, t):
                copy.wait_recv()

            def total(which, here, g=g, size=size):
                return keep[g][t, which, :, :, here] + rcv1[g][t, which, :, :, here].astype(jnp.int32).astype(
                    jnp.float32
                ) * scr[g][0, t, :, here].reshape(1, 1, size)

            def send(j, _, g=g, size=size, mine=mine):
                here = pl.ds(pl.multiple_of(j * size, size), size)
                codes, scale = coded(total(1 - mine, here).reshape(32, size))
                snd2[g][t, :, :, here] = codes.reshape(2, 16, size)
                scs[g][1, t, :, here] = scale
                return 0

            lax.fori_loop(0, width // size, send, 0)
            launch(t, functools.partial(sum_copy, 1, g))

            def hold(j, _, g=g, size=size, mine=mine):
                here = pl.ds(pl.multiple_of(j * size, size), size)
                keep[g][t, mine, :, :, here] = total(mine, here)
                return 0

            lax.fori_loop(0, width // size, hold, 0)

    def third(t):
        for g, (first, width, tiles) in enumerate(GROUPS):
            size = TILES[g]
            mine2, mine3 = dims[orders[g][1]][0], dims[orders[g][2]][0]
            for copy in sum_copy(1, g, t):
                copy.wait_recv()

            def total(which, here, g=g, size=size):
                return keep[g][t, mine2, which, :, here] + rcv2[g][t, which, :, here].astype(jnp.int32).astype(
                    jnp.float32
                ) * scr[g][1, t, :, here]

            def send(j, _, g=g, size=size, mine3=mine3):
                here = pl.ds(pl.multiple_of(j * size, size), size)
                codes, scale = coded(total(1 - mine3, here))
                snd3[g][t, :, here] = codes
                scs[g][2, t, :, here] = scale
                return 0

            lax.fori_loop(0, width // size, send, 0)
            launch(t, functools.partial(sum_copy, 2, g))

            def hold(j, _, g=g, size=size, mine2=mine2, mine3=mine3):
                here = pl.ds(pl.multiple_of(j * size, size), size)
                keep[g][t, mine2, mine3, :, here] = total(mine3, here)
                return 0

            lax.fori_loop(0, width // size, hold, 0)

    def fourth(t):
        step, rows = t // 4, pl.ds(pl.multiple_of((t % 4) * 8, 8), 8)
        for g, (first, width, tiles) in enumerate(GROUPS):
            size = TILES[g]
            mine2, mine3 = dims[orders[g][1]][0], dims[orders[g][2]][0]
            for copy in sum_copy(2, g, t):
                copy.wait_recv()

            def finish(j, _, g=g, size=size, first=first, mine2=mine2, mine3=mine3):
                here = pl.ds(pl.multiple_of(j * size, size), size)
                got = rcv3[g][t, :, here].astype(jnp.int32).astype(jnp.float32) * scr[g][2, t, :, here]
                total = keep[g][t, mine2, mine3, :, here] + got
                low, high = total[:8], total[8:]
                snd4[g][t, :, here] = jnp.where(core == 0, high, low)
                there = pl.ds(pl.multiple_of(core * HALF + first + j * size, size), size)
                out_ref[step, rows, there] = out_ref[step, rows, there] - jnp.where(core == 0, low, high)
                return 0

            lax.fori_loop(0, width // size, finish, 0)
            launch(t, lambda t, g=g: [last_copy(g, t)])

    def fifth(t):
        step, rows = t // 4, pl.ds(pl.multiple_of((t % 4) * 8, 8), 8)
        for g, (first, width, tiles) in enumerate(GROUPS):
            last_copy(g, t).wait_recv()
            there = pl.ds(pl.multiple_of((1 - core) * HALF + first, 128), width)
            out_ref[step, rows, there] = out_ref[step, rows, there] - rcv4[g][t]
        out_copy(t).start()

    def turn(i, _):
        def during(lag, body):
            @pl.when((i >= lag) & (i < lag + CHUNKS))
            def _():
                body(i - lag)

        @pl.when(i < LAG)
        def _():
            during(3, spread_3)
            during(2, spread_2)
            during(1, spread_1)
            during(0, spread_0)

        @pl.when(i == 0)
        def _():
            for j in range(4):
                remote_b(j).start()
            stiff_copy.start()
            mine_copy.wait()
            mask_copy.wait_recv()

        @pl.when(i < 2)
        def _():
            for j in range(2):
                local_b(2 * i + j).wait()
                mask_slice(0, mask_ref, 2 * i + j)

        @pl.when(i == 3)
        def _():
            for j in range(2):
                remote_b(j).wait_recv()
                mask_slice(1, mask2, j)

        during(LAG, product)

        @pl.when(i >= LAG)
        def _():
            during(0, spread_0)
            during(1, spread_1)
            during(2, spread_2)
            during(3, spread_3)

        @pl.when(i == LAG + 3)
        def _():
            stiff_copy.wait()

        during(LAG + 1, second)
        during(LAG + 2, third)
        during(LAG + 3, fourth)
        during(LAG + 4, fifth)
        return 0

    lax.fori_loop(0, CHUNKS + LAG + 4, turn, 0)

    mask_copy.wait_send()
    for i in range(4):
        remote_b(i).wait_send()

    def written(t, _):
        out_copy(t).wait()
        return 0

    lax.fori_loop(0, CHUNKS, written, 0)

    def drain(t, _):
        for stage in range(3):
            for g in range(3):
                for copy in sum_copy(stage, g, t):
                    copy.wait_send()
        for d in range(3):
            scatter(d, t).wait_send()
            gather(d, t).wait_send()
        cross(t).wait_send()
        twin_a(t).wait_send()
        for g in range(3):
            last_copy(g, t).wait_send()
        return 0

    lax.fori_loop(CHUNKS - SLOTS, CHUNKS, drain, 0)


def shards(interior, tile_mask, owner, stiffness):
    cand = pick(owner, interior, tile_mask)
    widths = [width for _, width, _ in GROUPS]

    def each(dtype, *lead):
        return tuple(pltpu.VMEM((*lead, width), dtype) for width in widths)

    f32, i16, bf16 = jnp.float32, jnp.int16, jnp.bfloat16
    dma = pltpu.SemaphoreType.DMA
    result = pl.pallas_call(
        main_kernel,
        out_shape=jax.ShapeDtypeStruct(stiffness.shape, f32),
        in_specs=[
            pl.BlockSpec(memory_space=pl.ANY),
            pl.BlockSpec(memory_space=pltpu.VMEM),
            pl.BlockSpec(memory_space=pl.ANY),
            pl.BlockSpec(memory_space=pl.ANY),
        ],
        out_specs=pl.BlockSpec(memory_space=pl.ANY),
        scratch_shapes=[
            pltpu.VMEM((STEPS, 32, 2 * HALF), f32),
            pltpu.VMEM((CHUNKS, 2, 16, DEPTH), bf16),
            pltpu.VMEM((2 * DEPTH, HALF), bf16),
            pltpu.VMEM((CHUNKS, 2, 8, 16, DEPTH), bf16),
            pltpu.VMEM((CHUNKS, 3, 2, 16, DEPTH), bf16),
            pltpu.VMEM((CHUNKS, 2, 16, DEPTH), bf16),
            pltpu.VMEM((CHUNKS, 2, 16, DEPTH), bf16),
            pltpu.VMEM((16, 128), jnp.int32),
            each(f32, CHUNKS, 2, 2, 16),
            each(i16, CHUNKS, 2, 2, 16),
            each(i16, CHUNKS, 2, 2, 16),
            each(i16, CHUNKS, 2, 16),
            each(i16, CHUNKS, 2, 16),
            each(i16, CHUNKS, 16),
            each(i16, CHUNKS, 16),
            each(f32, CHUNKS, 8),
            each(f32, CHUNKS, 8),
            each(f32, 3, CHUNKS, 1),
            each(f32, 3, CHUNKS, 1),
            dma((3, SLOTS)), dma((3, SLOTS)), dma((SLOTS,)), dma((SLOTS,)), dma((3, SLOTS)), dma((3, SLOTS)),
            dma((SLOTS,)), dma((SLOTS,)),
            dma((3, 3, SLOTS)), dma((3, 3, SLOTS)),
            dma((3, 3, SLOTS)), dma((3, 3, SLOTS)),
            dma((3, SLOTS)), dma((3, SLOTS)),
            dma((4,)), dma((4,)), dma((4,)),
            dma((1,)), dma((1,)), dma((1,)), dma((1,)), dma((CHUNKS,)),
        ],
        compiler_params=pltpu.CompilerParams(
            collective_id=0, has_side_effects=True, vmem_limit_bytes=62 * 1024 * 1024
        ),
    )(interior, tile_mask, cand, stiffness)
    return hand_over(result)


def solution(mesh):
    placed = (P("wide", "narrow"), P("wide", "narrow"), P(), P(None, "wide", "narrow"))
    return jax.shard_map(
        shards, mesh=mesh, in_specs=placed, out_specs=P(None, "wide", "narrow"), check_vma=False
    )
```

```python
import functools

import jax
import jax.numpy as jnp
from jax import lax
from jax.experimental import pallas as pl
from jax.experimental.pallas import tpu as pltpu
from jax.sharding import PartitionSpec as P

PW = 512
STEPS = 2
MESH = pl.DeviceIdType.MESH
CHUNKS = 8
SLOTS = 4
SENDS = 2
LAG = 4
HALF = 4096
DEPTH = 1024
GROUPS = ((0, 1792, (1024, 768)), (1792, 1408, (768, 640)), (3200, 896, (896,)))
TILES = (256, 128, 128)


def pick_kernel(owner_ref, w_hbm, mask_ref, out_hbm, order, blocks, turned, in_sem, out_sem):
    parts = [(step, part) for step in range(STEPS) for part in range(2)]

    def fetch(step, part):
        first = pl.multiple_of(owner_ref[step] % 16 * PW, PW)
        here = 2 * step + part
        return pltpu.make_async_copy(
            w_hbm.at[pl.ds(part * PW, PW), pl.ds(first, PW)], blocks.at[here], in_sem.at[here]
        )

    def leave(step, part):
        here = 2 * step + part
        return pltpu.make_async_copy(
            turned.at[here], out_hbm.at[pl.ds(4 * step, 4), :, :, pl.ds(part * PW, PW)], out_sem.at[here]
        )

    for step, part in parts:
        fetch(step, part).start()
    place = lax.broadcasted_iota(jnp.int32, (PW, 1), 0)
    source = lax.broadcasted_iota(jnp.int32, (PW, PW), 1)
    u, v, x = (place // 64) % 2, (place // 32) % 2, (place // 16) % 2
    y = 2 * u + (u + v) % 2
    origin = y * 128 + x * 64 + ((place // 8) % 2) * 32 + (place // 128) * 8 + place % 8
    order[...] = jnp.where(origin == source, 1.0, 0.0).astype(jnp.bfloat16)
    tile = lax.broadcasted_iota(jnp.int32, (128, PW), 0)
    column = lax.broadcasted_iota(jnp.int32, (1, PW), 1)
    rows = mask_ref[...].astype(jnp.float32).astype(jnp.bfloat16)
    for step in range(STEPS):
        own = owner_ref[step]
        held = own // 16 == lax.axis_index("narrow")
        wanted = jnp.where(held, (own % 16) * 8, -1000) + column // 64
        spread = jnp.where(tile == wanted, 1.0, 0.0).astype(jnp.bfloat16)
        mask = jnp.dot(rows, spread, preferred_element_type=jnp.float32)
        for part in range(2):
            here = 2 * step + part
            fetch(step, part).wait()
            pieces = []
            for i in range(8):
                row = 8 * part + i
                factor = jnp.broadcast_to(mask[row : row + 1, :], (16, PW)).astype(jnp.bfloat16)
                pieces += [blocks[here, k : k + 16, :] * factor for k in range(64 * i, 64 * i + 64, 16)]
            masked = jnp.concatenate(pieces, axis=0)
            product = lax.dot_general(
                order[...], masked, (((1,), (1,)), ((), ())), preferred_element_type=jnp.float32
            )
            turned[here] = product.astype(jnp.bfloat16).reshape(4, 8, 16, PW)
            leave(step, part).start()
    for step, part in parts:
        leave(step, part).wait()


def pick(owner, interior, tile_mask):
    return pl.pallas_call(
        pick_kernel,
        out_shape=jax.ShapeDtypeStruct((CHUNKS, 8, 16, DEPTH), jnp.bfloat16),
        in_specs=[
            pl.BlockSpec(memory_space=pltpu.SMEM),
            pl.BlockSpec(memory_space=pl.ANY),
            pl.BlockSpec(memory_space=pltpu.VMEM),
        ],
        out_specs=pl.BlockSpec(memory_space=pl.ANY),
        scratch_shapes=[
            pltpu.VMEM((PW, PW), jnp.bfloat16),
            pltpu.VMEM((4, PW, PW), jnp.bfloat16),
            pltpu.VMEM((4, 4, 8, 16, PW), jnp.bfloat16),
            pltpu.SemaphoreType.DMA((4,)),
            pltpu.SemaphoreType.DMA((4,)),
        ],
    )(owner, interior, tile_mask)


def hand_over_kernel(source, target, buffer, in_sem, out_sem):
    def move(t, inward):
        rows = pl.ds((t % 4) * 8, 8)
        if inward:
            return pltpu.make_async_copy(source.at[t // 4, rows], buffer.at[t], in_sem.at[t])
        return pltpu.make_async_copy(buffer.at[t], target.at[t // 4, rows], out_sem.at[t])

    for t in range(CHUNKS):
        move(t, True).start()
    for t in range(CHUNKS):
        move(t, True).wait()
        move(t, False).start()
    for t in range(CHUNKS):
        move(t, False).wait()


def hand_over(result):
    return pl.pallas_call(
        hand_over_kernel,
        out_shape=jax.ShapeDtypeStruct(result.shape, result.dtype),
        in_specs=[pl.BlockSpec(memory_space=pl.ANY)],
        out_specs=pl.BlockSpec(memory_space=pl.ANY),
        scratch_shapes=[
            pltpu.VMEM((CHUNKS, 8, 2 * HALF), jnp.float32),
            pltpu.SemaphoreType.DMA((CHUNKS,)),
            pltpu.SemaphoreType.DMA((CHUNKS,)),
        ],
    )(result)


def coded(values):
    most = jnp.maximum(jnp.max(jnp.abs(values), axis=0, keepdims=True), 1e-30)
    codes = jnp.round(values * (32767.0 / most)).astype(jnp.int32).astype(jnp.int16)
    return codes, most * (1.0 / 32767.0)


def main_kernel(
    w_hbm, mask_ref, cand, stiff_hbm, out_hbm,
    out_ref, mine_c, b, a, r1, s1, r2, mask2, keep, snd1, rcv1, snd2, rcv2, snd3, rcv3, snd4, rcv4, scs, scr,
    c1_s, c1_r, c2_s, c2_r, c3_s, c3_r, ac_s, ac_r, rd_s, rd_r, rs_s, rs_r, o_s, o_r, bl_s, br_s, br_r, m_s, m_r, st_s, mc_s, w_s,
):
    w, n = lax.axis_index("wide"), lax.axis_index("narrow")
    core, x, y = w % 2, (w // 2) % 2, w // 4
    z, h = n // 2, n % 2
    u = y // 2
    v = (u + y % 2) % 2

    def at(y, x, core):
        return ((y * 2 + x) * 2 + core, n)

    twin = at(y, x, 1 - core)
    dims = {"v": (v, at(y + 1 - 2 * (y % 2), x, core)), "u": (u, at(3 - y, x, core)), "x": (x, at(y, 1 - x, core))}
    orders = ("vux", "uxv", "xvu")
    others = [(z + d) % 4 for d in (1, 2, 3)]
    ring = [(w, other * 2 + h) for other in others]
    across = (w, z * 2 + 1 - h)

    def remote(src, dst, s, r, device):
        return pltpu.make_async_remote_copy(
            src_ref=src, dst_ref=dst, send_sem=s, recv_sem=r, device_id=device, device_id_type=MESH
        )

    barrier = pltpu.get_barrier_semaphore()
    peers = (twin, dims["v"][1], dims["u"][1], dims["x"][1], *ring, across)
    for peer in peers:
        pl.semaphore_signal(barrier, inc=1, device_id=peer, device_id_type=MESH)

    def local_b(i):
        first = pl.multiple_of(core * HALF + i * 1024, 1024)
        return pltpu.make_async_copy(
            w_hbm.at[:, pl.ds(first, 1024)],
            b.at[pl.ds(0, DEPTH), pl.ds(pl.multiple_of(i * 1024, 1024), 1024)],
            bl_s.at[i],
        )

    def remote_b(i):
        first = pl.multiple_of((1 - core) * HALF + i * 1024, 1024)
        return remote(
            w_hbm.at[:, pl.ds(first, 1024)],
            b.at[pl.ds(DEPTH, DEPTH), pl.ds(pl.multiple_of(i * 1024, 1024), 1024)],
            br_s.at[i], br_r.at[i], twin,
        )

    mask_copy = remote(mask_ref, mask2, m_s.at[0], m_r.at[0], twin)
    stiff_copy = pltpu.make_async_copy(stiff_hbm, out_ref, st_s.at[0])
    mine_copy = pltpu.make_async_copy(cand.at[:, pl.ds(2 * z, 2)], mine_c, mc_s.at[0])

    def out_copy(t):
        rows = pl.ds(pl.multiple_of((t % 4) * 8, 8), 8)
        return pltpu.make_async_copy(out_ref.at[t // 4, rows], out_hbm.at[t // 4, rows], w_s.at[t])


    def quarter(z):
        return pl.ds(2 * z, 2)

    def piece(p):
        return pl.ds(p * (DEPTH // 2), DEPTH // 2)

    def scatter(p, d, t):
        return remote(
            cand.at[t, quarter(others[d]), :, piece(p)], r1.at[t, d, :, :, piece(p)],
            c1_s.at[p, d, t % SENDS], c1_r.at[p, d, t % SLOTS], ring[d],
        )

    def cross(p, t):
        return remote(
            s1.at[t, :, :, piece(p)], r2.at[t, :, :, piece(p)],
            c2_s.at[p, t % SENDS], c2_r.at[p, t % SLOTS], across,
        )

    def gather(p, d, t):
        part = a.at[t, 0, quarter(z), :, piece(p)]
        return remote(part, part, c3_s.at[p, d, t % SENDS], c3_r.at[p, d, t % SLOTS], ring[d])

    def twin_a(p, t):
        return remote(
            a.at[t, 0, :, :, piece(p)], a.at[t, 1, :, :, piece(p)],
            ac_s.at[p, t % SENDS], ac_r.at[p, t % SLOTS], twin,
        )

    def sum_copy(stage, g, t):
        src = (snd1, snd2, snd3)[stage][g]
        dst = (rcv1, rcv2, rcv3)[stage][g]
        peer = dims[orders[g][stage]][1]
        slot, sent = t % SLOTS, t % SENDS
        return (
            remote(src.at[t], dst.at[t], rd_s.at[stage, g, sent], rd_r.at[stage, g, slot], peer),
            remote(scs[g].at[stage, t], scr[g].at[stage, t], rs_s.at[stage, g, sent], rs_r.at[stage, g, slot], peer),
        )

    def last_copy(g, t):
        return remote(snd4[g].at[t], rcv4[g].at[t], o_s.at[g, t % SENDS], o_r.at[g, t % SLOTS], twin)

    mine_copy.start()
    for i in range(4):
        local_b(i).start()
    pl.semaphore_wait(barrier, len(peers))
    mask_copy.start()

    def launch(t, copies):
        @pl.when(t >= SENDS)
        def _():
            for copy in copies(t - SENDS):
                copy.wait_send()

        for copy in copies(t):
            copy.start()

    def scatters(p, t):
        return [scatter(p, d, t) for d in range(3)]

    def gathers(p, t):
        return [gather(p, d, t) for d in range(3)]

    def spread_0(t):
        for p in range(2):
            launch(t, functools.partial(scatters, p))

    def spread_1(t):
        for p in range(2):
            for copy in scatters(p, t):
                copy.wait_recv()
            cols = piece(p)
            s1[t, :, :, cols] = (mine_c[t, :, :, cols] + r1[t, 0, :, :, cols]) + (
                r1[t, 1, :, :, cols] + r1[t, 2, :, :, cols]
            )
            launch(t, lambda t, p=p: [cross(p, t)])

    def spread_2(t):
        for p in range(2):
            cross(p, t).wait_recv()
            cols = piece(p)
            a[t, 0, quarter(z), :, cols] = s1[t, :, :, cols] + r2[t, :, :, cols]
            launch(t, functools.partial(gathers, p))

    def spread_3(t):
        for p in range(2):
            for copy in gathers(p, t):
                copy.wait_recv()
            launch(t, lambda t, p=p: [twin_a(p, t)])

    def mask_slice(half, ref, i):
        cols = pl.ds(pl.multiple_of(i * 1024, 1024), 1024)
        tile = lax.broadcasted_iota(jnp.int32, (128, 1024), 0)
        column = lax.broadcasted_iota(jnp.int32, (1, 1024), 1)
        wanted = core * 64 + i * 16 + column // 64
        spread = jnp.where(tile == wanted, 1.0, 0.0).astype(jnp.bfloat16)
        rows = ref[...].astype(jnp.float32).astype(jnp.bfloat16)
        mask = jnp.dot(rows, spread, preferred_element_type=jnp.float32)
        for k in range(16):
            factor = jnp.broadcast_to(mask[k : k + 1, :], (16, 1024)).astype(jnp.bfloat16)
            for row in range(half * DEPTH + 64 * k, half * DEPTH + 64 * k + 64, 16):
                b[row : row + 16, cols] = b[row : row + 16, cols] * factor

    def product(t):
        for p in range(2):
            twin_a(p, t).wait_recv()
        for g, (first, width, tiles) in enumerate(GROUPS):
            if g == 1:

                @pl.when(t == 0)
                def _():
                    for j in (2, 3):
                        remote_b(j).wait_recv()
                        mask_slice(1, mask2, j)

            names = orders[g]
            mine = dims[names[0]][0]

            def block(bit, second, third):
                bits = {names[0]: bit, names[1]: second, names[2]: third}
                index = bits["u"] * 4 + bits["v"] * 2 + bits["x"]
                return jnp.concatenate([a[t, 0, index], a[t, 1, index]], axis=1)

            lhs = jnp.concatenate(
                [block(bit, j, k) for bit in (1 - mine, mine) for j in (0, 1) for k in (0, 1)], axis=0
            )
            done = 0
            for size in tiles:
                here = pl.ds(done, size)
                both = jnp.dot(lhs, b[:, pl.ds(first + done, size)], preferred_element_type=jnp.float32)
                codes, scale = coded(both[:64])
                snd1[g][t, :, :, :, here] = codes.reshape(2, 2, 16, size)
                scs[g][0, t, :, here] = scale
                keep[g][t, :, :, :, here] = both[64:].reshape(2, 2, 16, size)
                done += size
            launch(t, functools.partial(sum_copy, 0, g))

    def second(t):
        for g, (first, width, tiles) in enumerate(GROUPS):
            size = TILES[g]
            mine = dims[orders[g][1]][0]
            for copy in sum_copy(0, g, t):
                copy.wait_recv()

            def total(which, here, g=g, size=size):
                return keep[g][t, which, :, :, here] + rcv1[g][t, which, :, :, here].astype(jnp.int32).astype(
                    jnp.float32
                ) * scr[g][0, t, :, here].reshape(1, 1, size)

            def send(j, _, g=g, size=size, mine=mine):
                here = pl.ds(pl.multiple_of(j * size, size), size)
                codes, scale = coded(total(1 - mine, here).reshape(32, size))
                snd2[g][t, :, :, here] = codes.reshape(2, 16, size)
                scs[g][1, t, :, here] = scale
                return 0

            lax.fori_loop(0, width // size, send, 0)
            launch(t, functools.partial(sum_copy, 1, g))

            def hold(j, _, g=g, size=size, mine=mine):
                here = pl.ds(pl.multiple_of(j * size, size), size)
                keep[g][t, mine, :, :, here] = total(mine, here)
                return 0

            lax.fori_loop(0, width // size, hold, 0)

    def third(t):
        for g, (first, width, tiles) in enumerate(GROUPS):
            size = TILES[g]
            mine2, mine3 = dims[orders[g][1]][0], dims[orders[g][2]][0]
            for copy in sum_copy(1, g, t):
                copy.wait_recv()

            def total(which, here, g=g, size=size):
                return keep[g][t, mine2, which, :, here] + rcv2[g][t, which, :, here].astype(jnp.int32).astype(
                    jnp.float32
                ) * scr[g][1, t, :, here]

            def send(j, _, g=g, size=size, mine3=mine3):
                here = pl.ds(pl.multiple_of(j * size, size), size)
                codes, scale = coded(total(1 - mine3, here))
                snd3[g][t, :, here] = codes
                scs[g][2, t, :, here] = scale
                return 0

            lax.fori_loop(0, width // size, send, 0)
            launch(t, functools.partial(sum_copy, 2, g))

            def hold(j, _, g=g, size=size, mine2=mine2, mine3=mine3):
                here = pl.ds(pl.multiple_of(j * size, size), size)
                keep[g][t, mine2, mine3, :, here] = total(mine3, here)
                return 0

            lax.fori_loop(0, width // size, hold, 0)

    def fourth(t):
        step, rows = t // 4, pl.ds(pl.multiple_of((t % 4) * 8, 8), 8)
        for g, (first, width, tiles) in enumerate(GROUPS):
            size = TILES[g]
            mine2, mine3 = dims[orders[g][1]][0], dims[orders[g][2]][0]
            for copy in sum_copy(2, g, t):
                copy.wait_recv()

            def finish(j, _, g=g, size=size, first=first, mine2=mine2, mine3=mine3):
                here = pl.ds(pl.multiple_of(j * size, size), size)
                got = rcv3[g][t, :, here].astype(jnp.int32).astype(jnp.float32) * scr[g][2, t, :, here]
                total = keep[g][t, mine2, mine3, :, here] + got
                low, high = total[:8], total[8:]
                snd4[g][t, :, here] = jnp.where(core == 0, high, low)
                there = pl.ds(pl.multiple_of(core * HALF + first + j * size, size), size)
                out_ref[step, rows, there] = out_ref[step, rows, there] - jnp.where(core == 0, low, high)
                return 0

            lax.fori_loop(0, width // size, finish, 0)
            launch(t, lambda t, g=g: [last_copy(g, t)])

    def fifth(t):
        step, rows = t // 4, pl.ds(pl.multiple_of((t % 4) * 8, 8), 8)
        for g, (first, width, tiles) in enumerate(GROUPS):
            last_copy(g, t).wait_recv()
            there = pl.ds(pl.multiple_of((1 - core) * HALF + first, 128), width)
            out_ref[step, rows, there] = out_ref[step, rows, there] - rcv4[g][t]
        out_copy(t).start()

    def turn(i, _):
        def during(lag, body):
            @pl.when((i >= lag) & (i < lag + CHUNKS))
            def _():
                body(i - lag)

        @pl.when(i < LAG)
        def _():
            during(3, spread_3)
            during(2, spread_2)
            during(1, spread_1)
            during(0, spread_0)

        @pl.when(i == 0)
        def _():
            for j in range(4):
                remote_b(j).start()
            stiff_copy.start()
            mine_copy.wait()
            mask_copy.wait_recv()

        def own_slice(j):
            local_b(j).wait()
            mask_slice(0, mask_ref, j)

        def other_slice(j):
            remote_b(j).wait_recv()
            mask_slice(1, mask2, j)

        @pl.when(i < 3)
        def _():
            own_slice(i)

        @pl.when(i == 0)
        def _():
            own_slice(3)

        @pl.when((i >= 2) & (i < 4))
        def _():
            other_slice(i - 2)

        during(LAG, product)

        @pl.when(i >= LAG)
        def _():
            during(0, spread_0)
            during(1, spread_1)
            during(2, spread_2)
            during(3, spread_3)

        @pl.when(i == LAG + 3)
        def _():
            stiff_copy.wait()

        during(LAG + 1, second)
        during(LAG + 2, third)
        during(LAG + 3, fourth)
        during(LAG + 4, fifth)
        return 0

    lax.fori_loop(0, CHUNKS + LAG + 4, turn, 0)

    mask_copy.wait_send()
    for i in range(4):
        remote_b(i).wait_send()

    def written(t, _):
        out_copy(t).wait()
        return 0

    lax.fori_loop(0, CHUNKS, written, 0)

    def drain(t, _):
        for stage in range(3):
            for g in range(3):
                for copy in sum_copy(stage, g, t):
                    copy.wait_send()
        for p in range(2):
            for copy in (*scatters(p, t), *gathers(p, t), cross(p, t), twin_a(p, t)):
                copy.wait_send()
        for g in range(3):
            last_copy(g, t).wait_send()
        return 0

    lax.fori_loop(CHUNKS - SENDS, CHUNKS, drain, 0)


def shards(interior, tile_mask, owner, stiffness):
    cand = pick(owner, interior, tile_mask)
    widths = [width for _, width, _ in GROUPS]

    def each(dtype, *lead):
        return tuple(pltpu.VMEM((*lead, width), dtype) for width in widths)

    f32, i16, bf16 = jnp.float32, jnp.int16, jnp.bfloat16
    dma = pltpu.SemaphoreType.DMA
    result = pl.pallas_call(
        main_kernel,
        out_shape=jax.ShapeDtypeStruct(stiffness.shape, f32),
        in_specs=[
            pl.BlockSpec(memory_space=pl.ANY),
            pl.BlockSpec(memory_space=pltpu.VMEM),
            pl.BlockSpec(memory_space=pl.ANY),
            pl.BlockSpec(memory_space=pl.ANY),
        ],
        out_specs=pl.BlockSpec(memory_space=pl.ANY),
        scratch_shapes=[
            pltpu.VMEM((STEPS, 32, 2 * HALF), f32),
            pltpu.VMEM((CHUNKS, 2, 16, DEPTH), bf16),
            pltpu.VMEM((2 * DEPTH, HALF), bf16),
            pltpu.VMEM((CHUNKS, 2, 8, 16, DEPTH), bf16),
            pltpu.VMEM((CHUNKS, 3, 2, 16, DEPTH), bf16),
            pltpu.VMEM((CHUNKS, 2, 16, DEPTH), bf16),
            pltpu.VMEM((CHUNKS, 2, 16, DEPTH), bf16),
            pltpu.VMEM((16, 128), jnp.int32),
            each(f32, CHUNKS, 2, 2, 16),
            each(i16, CHUNKS, 2, 2, 16),
            each(i16, CHUNKS, 2, 2, 16),
            each(i16, CHUNKS, 2, 16),
            each(i16, CHUNKS, 2, 16),
            each(i16, CHUNKS, 16),
            each(i16, CHUNKS, 16),
            each(f32, CHUNKS, 8),
            each(f32, CHUNKS, 8),
            each(f32, 3, CHUNKS, 1),
            each(f32, 3, CHUNKS, 1),
            dma((2, 3, SENDS)), dma((2, 3, SLOTS)), dma((2, SENDS)), dma((2, SLOTS)),
            dma((2, 3, SENDS)), dma((2, 3, SLOTS)), dma((2, SENDS)), dma((2, SLOTS)),
            dma((3, 3, SENDS)), dma((3, 3, SLOTS)),
            dma((3, 3, SENDS)), dma((3, 3, SLOTS)),
            dma((3, SENDS)), dma((3, SLOTS)),
            dma((4,)), dma((4,)), dma((4,)),
            dma((1,)), dma((1,)), dma((1,)), dma((1,)), dma((CHUNKS,)),
        ],
        compiler_params=pltpu.CompilerParams(
            collective_id=0, has_side_effects=True, vmem_limit_bytes=62 * 1024 * 1024
        ),
    )(interior, tile_mask, cand, stiffness)
    return hand_over(result)


def solution(mesh):
    placed = (P("wide", "narrow"), P("wide", "narrow"), P(), P(None, "wide", "narrow"))
    return jax.shard_map(
        shards, mesh=mesh, in_specs=placed, out_specs=P(None, "wide", "narrow"), check_vma=False
    )
```

```python
import functools

import jax
import jax.numpy as jnp
from jax import lax
from jax.experimental import pallas as pl
from jax.experimental.pallas import tpu as pltpu
from jax.sharding import PartitionSpec as P

PW = 512
STEPS = 2
MESH = pl.DeviceIdType.MESH
CHUNKS = 8
SLOTS = 4
SENDS = 2
LAG = 4
HALF = 4096
DEPTH = 1024
GROUPS = ((0, 1792, (1024, 768)), (1792, 1408, (768, 640)), (3200, 896, (896,)))
TILES = (896, 1408, 896)


def pick_kernel(owner_ref, w_hbm, mask_ref, out_hbm, order, blocks, turned, in_sem, out_sem):
    parts = [(step, part) for step in range(STEPS) for part in range(2)]

    def fetch(step, part):
        first = pl.multiple_of(owner_ref[step] % 16 * PW, PW)
        here = 2 * step + part
        return pltpu.make_async_copy(
            w_hbm.at[pl.ds(part * PW, PW), pl.ds(first, PW)], blocks.at[here], in_sem.at[here]
        )

    def leave(step, part):
        here = 2 * step + part
        return pltpu.make_async_copy(
            turned.at[here], out_hbm.at[pl.ds(4 * step, 4), :, :, pl.ds(part * PW, PW)], out_sem.at[here]
        )

    for step, part in parts:
        fetch(step, part).start()
    place = lax.broadcasted_iota(jnp.int32, (PW, 1), 0)
    source = lax.broadcasted_iota(jnp.int32, (PW, PW), 1)
    u, v, x = (place // 64) % 2, (place // 32) % 2, (place // 16) % 2
    y = 2 * u + (u + v) % 2
    origin = y * 128 + x * 64 + ((place // 8) % 2) * 32 + (place // 128) * 8 + place % 8
    order[...] = jnp.where(origin == source, 1.0, 0.0).astype(jnp.bfloat16)
    tile = lax.broadcasted_iota(jnp.int32, (128, PW), 0)
    column = lax.broadcasted_iota(jnp.int32, (1, PW), 1)
    rows = mask_ref[...].astype(jnp.float32).astype(jnp.bfloat16)
    for step in range(STEPS):
        own = owner_ref[step]
        held = own // 16 == lax.axis_index("narrow")
        wanted = jnp.where(held, (own % 16) * 8, -1000) + column // 64
        spread = jnp.where(tile == wanted, 1.0, 0.0).astype(jnp.bfloat16)
        mask = jnp.dot(rows, spread, preferred_element_type=jnp.float32)
        for part in range(2):
            here = 2 * step + part
            fetch(step, part).wait()
            pieces = []
            for i in range(8):
                row = 8 * part + i
                factor = jnp.broadcast_to(mask[row : row + 1, :], (16, PW)).astype(jnp.bfloat16)
                pieces += [blocks[here, k : k + 16, :] * factor for k in range(64 * i, 64 * i + 64, 16)]
            masked = jnp.concatenate(pieces, axis=0)
            product = lax.dot_general(
                order[...], masked, (((1,), (1,)), ((), ())), preferred_element_type=jnp.float32
            )
            turned[here] = product.astype(jnp.bfloat16).reshape(4, 8, 16, PW)
            leave(step, part).start()
    for step, part in parts:
        leave(step, part).wait()


def pick(owner, interior, tile_mask):
    return pl.pallas_call(
        pick_kernel,
        out_shape=jax.ShapeDtypeStruct((CHUNKS, 8, 16, DEPTH), jnp.bfloat16),
        in_specs=[
            pl.BlockSpec(memory_space=pltpu.SMEM),
            pl.BlockSpec(memory_space=pl.ANY),
            pl.BlockSpec(memory_space=pltpu.VMEM),
        ],
        out_specs=pl.BlockSpec(memory_space=pl.ANY),
        scratch_shapes=[
            pltpu.VMEM((PW, PW), jnp.bfloat16),
            pltpu.VMEM((4, PW, PW), jnp.bfloat16),
            pltpu.VMEM((4, 4, 8, 16, PW), jnp.bfloat16),
            pltpu.SemaphoreType.DMA((4,)),
            pltpu.SemaphoreType.DMA((4,)),
        ],
    )(owner, interior, tile_mask)


def hand_over_kernel(source, target, buffer, in_sem, out_sem):
    def move(t, inward):
        rows = pl.ds((t % 4) * 8, 8)
        if inward:
            return pltpu.make_async_copy(source.at[t // 4, rows], buffer.at[t], in_sem.at[t])
        return pltpu.make_async_copy(buffer.at[t], target.at[t // 4, rows], out_sem.at[t])

    for t in range(CHUNKS):
        move(t, True).start()
    for t in range(CHUNKS):
        move(t, True).wait()
        move(t, False).start()
    for t in range(CHUNKS):
        move(t, False).wait()


def hand_over(result):
    return pl.pallas_call(
        hand_over_kernel,
        out_shape=jax.ShapeDtypeStruct(result.shape, result.dtype),
        in_specs=[pl.BlockSpec(memory_space=pl.ANY)],
        out_specs=pl.BlockSpec(memory_space=pl.ANY),
        scratch_shapes=[
            pltpu.VMEM((CHUNKS, 8, 2 * HALF), jnp.float32),
            pltpu.SemaphoreType.DMA((CHUNKS,)),
            pltpu.SemaphoreType.DMA((CHUNKS,)),
        ],
    )(result)


def coded(values):
    most = jnp.maximum(jnp.max(jnp.abs(values), axis=0, keepdims=True), 1e-30)
    codes = jnp.round(values * (32767.0 / most)).astype(jnp.int32).astype(jnp.int16)
    return codes, most * (1.0 / 32767.0)


def main_kernel(
    w_hbm, mask_ref, cand, stiff_hbm, out_hbm,
    out_ref, mine_c, b, a, r1, s1, r2, mask2, keep, snd1, rcv1, snd2, rcv2, snd3, rcv3, snd4, rcv4, scs, scr,
    c1_s, c1_r, c2_s, c2_r, c3_s, c3_r, ac_s, ac_r, rd_s, rd_r, rs_s, rs_r, o_s, o_r, bl_s, br_s, br_r, m_s, m_r, st_s, mc_s, w_s,
):
    w, n = lax.axis_index("wide"), lax.axis_index("narrow")
    core, x, y = w % 2, (w // 2) % 2, w // 4
    z, h = n // 2, n % 2
    u = y // 2
    v = (u + y % 2) % 2

    def at(y, x, core):
        return ((y * 2 + x) * 2 + core, n)

    twin = at(y, x, 1 - core)
    dims = {"v": (v, at(y + 1 - 2 * (y % 2), x, core)), "u": (u, at(3 - y, x, core)), "x": (x, at(y, 1 - x, core))}
    orders = ("vux", "uxv", "xvu")
    others = [(z + d) % 4 for d in (1, 2, 3)]
    ring = [(w, other * 2 + h) for other in others]
    across = (w, z * 2 + 1 - h)

    def remote(src, dst, s, r, device):
        return pltpu.make_async_remote_copy(
            src_ref=src, dst_ref=dst, send_sem=s, recv_sem=r, device_id=device, device_id_type=MESH
        )

    barrier = pltpu.get_barrier_semaphore()
    peers = (twin, dims["v"][1], dims["u"][1], dims["x"][1], *ring, across)
    for peer in peers:
        pl.semaphore_signal(barrier, inc=1, device_id=peer, device_id_type=MESH)

    def local_b(i):
        first = pl.multiple_of(core * HALF + i * 1024, 1024)
        return pltpu.make_async_copy(
            w_hbm.at[:, pl.ds(first, 1024)],
            b.at[pl.ds(0, DEPTH), pl.ds(pl.multiple_of(i * 1024, 1024), 1024)],
            bl_s.at[i],
        )

    def remote_b(i):
        first = pl.multiple_of((1 - core) * HALF + i * 1024, 1024)
        return remote(
            w_hbm.at[:, pl.ds(first, 1024)],
            b.at[pl.ds(DEPTH, DEPTH), pl.ds(pl.multiple_of(i * 1024, 1024), 1024)],
            br_s.at[i], br_r.at[i], twin,
        )

    mask_copy = remote(mask_ref, mask2, m_s.at[0], m_r.at[0], twin)
    stiff_copy = pltpu.make_async_copy(stiff_hbm, out_ref, st_s.at[0])
    mine_copy = pltpu.make_async_copy(cand.at[:, pl.ds(2 * z, 2)], mine_c, mc_s.at[0])

    def out_copy(t):
        rows = pl.ds(pl.multiple_of((t % 4) * 8, 8), 8)
        return pltpu.make_async_copy(out_ref.at[t // 4, rows], out_hbm.at[t // 4, rows], w_s.at[t])


    def quarter(z):
        return pl.ds(2 * z, 2)

    def piece(p):
        return pl.ds(p * (DEPTH // 2), DEPTH // 2)

    def scatter(p, d, t):
        return remote(
            cand.at[t, quarter(others[d]), :, piece(p)], r1.at[t, d, :, :, piece(p)],
            c1_s.at[p, d, t % SENDS], c1_r.at[p, d, t % SLOTS], ring[d],
        )

    def cross(p, t):
        return remote(
            s1.at[t, :, :, piece(p)], r2.at[t, :, :, piece(p)],
            c2_s.at[p, t % SENDS], c2_r.at[p, t % SLOTS], across,
        )

    def gather(p, d, t):
        part = a.at[t, 0, quarter(z), :, piece(p)]
        return remote(part, part, c3_s.at[p, d, t % SENDS], c3_r.at[p, d, t % SLOTS], ring[d])

    def twin_a(p, t):
        return remote(
            a.at[t, 0, :, :, piece(p)], a.at[t, 1, :, :, piece(p)],
            ac_s.at[p, t % SENDS], ac_r.at[p, t % SLOTS], twin,
        )

    def sum_copy(stage, g, t):
        src = (snd1, snd2, snd3)[stage][g]
        dst = (rcv1, rcv2, rcv3)[stage][g]
        peer = dims[orders[g][stage]][1]
        slot, sent = t % SLOTS, t % SENDS
        return (
            remote(src.at[t], dst.at[t], rd_s.at[stage, g, sent], rd_r.at[stage, g, slot], peer),
            remote(scs[g].at[stage, t], scr[g].at[stage, t], rs_s.at[stage, g, sent], rs_r.at[stage, g, slot], peer),
        )

    def last_copy(g, t):
        return remote(snd4[g].at[t], rcv4[g].at[t], o_s.at[g, t % SENDS], o_r.at[g, t % SLOTS], twin)

    mine_copy.start()
    for i in range(4):
        local_b(i).start()
    pl.semaphore_wait(barrier, len(peers))
    mask_copy.start()

    def launch(t, copies):
        @pl.when(t >= SENDS)
        def _():
            for copy in copies(t - SENDS):
                copy.wait_send()

        for copy in copies(t):
            copy.start()

    def scatters(p, t):
        return [scatter(p, d, t) for d in range(3)]

    def gathers(p, t):
        return [gather(p, d, t) for d in range(3)]

    def spread_0(t):
        for p in range(2):
            launch(t, functools.partial(scatters, p))

    def spread_1(t):
        for p in range(2):
            for copy in scatters(p, t):
                copy.wait_recv()
            cols = piece(p)
            s1[t, :, :, cols] = (mine_c[t, :, :, cols] + r1[t, 0, :, :, cols]) + (
                r1[t, 1, :, :, cols] + r1[t, 2, :, :, cols]
            )
            launch(t, lambda t, p=p: [cross(p, t)])

    def spread_2(t):
        for p in range(2):
            cross(p, t).wait_recv()
            cols = piece(p)
            a[t, 0, quarter(z), :, cols] = s1[t, :, :, cols] + r2[t, :, :, cols]
            launch(t, functools.partial(gathers, p))

    def spread_3(t):
        for p in range(2):
            for copy in gathers(p, t):
                copy.wait_recv()
            launch(t, lambda t, p=p: [twin_a(p, t)])

    def mask_slice(half, ref, i):
        cols = pl.ds(pl.multiple_of(i * 1024, 1024), 1024)
        tile = lax.broadcasted_iota(jnp.int32, (128, 1024), 0)
        column = lax.broadcasted_iota(jnp.int32, (1, 1024), 1)
        wanted = core * 64 + i * 16 + column // 64
        spread = jnp.where(tile == wanted, 1.0, 0.0).astype(jnp.bfloat16)
        rows = ref[...].astype(jnp.float32).astype(jnp.bfloat16)
        mask = jnp.dot(rows, spread, preferred_element_type=jnp.float32)
        for k in range(16):
            factor = jnp.broadcast_to(mask[k : k + 1, :], (16, 1024)).astype(jnp.bfloat16)
            for row in range(half * DEPTH + 64 * k, half * DEPTH + 64 * k + 64, 16):
                b[row : row + 16, cols] = b[row : row + 16, cols] * factor

    def product(t):
        for p in range(2):
            twin_a(p, t).wait_recv()
        for g, (first, width, tiles) in enumerate(GROUPS):
            if g == 1:

                @pl.when(t == 0)
                def _():
                    for j in (2, 3):
                        remote_b(j).wait_recv()
                        mask_slice(1, mask2, j)

            names = orders[g]
            mine = dims[names[0]][0]

            def block(bit, second, third):
                bits = {names[0]: bit, names[1]: second, names[2]: third}
                index = bits["u"] * 4 + bits["v"] * 2 + bits["x"]
                return jnp.concatenate([a[t, 0, index], a[t, 1, index]], axis=1)

            lhs = jnp.concatenate(
                [block(bit, j, k) for bit in (1 - mine, mine) for j in (0, 1) for k in (0, 1)], axis=0
            )
            done = 0
            for size in tiles:
                here = pl.ds(done, size)
                both = jnp.dot(lhs, b[:, pl.ds(first + done, size)], preferred_element_type=jnp.float32)
                codes, scale = coded(both[:64])
                snd1[g][t, :, :, :, here] = codes.reshape(2, 2, 16, size)
                scs[g][0, t, :, here] = scale
                keep[g][t, :, :, :, here] = both[64:].reshape(2, 2, 16, size)
                done += size
            launch(t, functools.partial(sum_copy, 0, g))

    def sweep(count, body):
        for j in range(count):
            body(j)

    def second(t):
        for g, (first, width, tiles) in enumerate(GROUPS):
            size = TILES[g]
            mine = dims[orders[g][1]][0]
            for copy in sum_copy(0, g, t):
                copy.wait_recv()

            def total(which, here, g=g, size=size):
                return keep[g][t, which, :, :, here] + rcv1[g][t, which, :, :, here].astype(jnp.int32).astype(
                    jnp.float32
                ) * scr[g][0, t, :, here].reshape(1, 1, size)

            def send(j, g=g, size=size, mine=mine):
                here = pl.ds(j * size, size)
                codes, scale = coded(total(1 - mine, here).reshape(32, size))
                snd2[g][t, :, :, here] = codes.reshape(2, 16, size)
                scs[g][1, t, :, here] = scale
                return 0

            sweep(width // size, send)
            launch(t, functools.partial(sum_copy, 1, g))

            def hold(j, g=g, size=size, mine=mine):
                here = pl.ds(j * size, size)
                keep[g][t, mine, :, :, here] = total(mine, here)
                return 0

            sweep(width // size, hold)

    def third(t):
        for g, (first, width, tiles) in enumerate(GROUPS):
            size = TILES[g]
            mine2, mine3 = dims[orders[g][1]][0], dims[orders[g][2]][0]
            for copy in sum_copy(1, g, t):
                copy.wait_recv()

            def total(which, here, g=g, size=size):
                return keep[g][t, mine2, which, :, here] + rcv2[g][t, which, :, here].astype(jnp.int32).astype(
                    jnp.float32
                ) * scr[g][1, t, :, here]

            def send(j, g=g, size=size, mine3=mine3):
                here = pl.ds(j * size, size)
                codes, scale = coded(total(1 - mine3, here))
                snd3[g][t, :, here] = codes
                scs[g][2, t, :, here] = scale
                return 0

            sweep(width // size, send)
            launch(t, functools.partial(sum_copy, 2, g))

            def hold(j, g=g, size=size, mine2=mine2, mine3=mine3):
                here = pl.ds(j * size, size)
                keep[g][t, mine2, mine3, :, here] = total(mine3, here)
                return 0

            sweep(width // size, hold)

    def fourth(t):
        step, rows = t // 4, pl.ds(pl.multiple_of((t % 4) * 8, 8), 8)
        for g, (first, width, tiles) in enumerate(GROUPS):
            size = TILES[g]
            mine2, mine3 = dims[orders[g][1]][0], dims[orders[g][2]][0]
            for copy in sum_copy(2, g, t):
                copy.wait_recv()

            def finish(j, g=g, size=size, first=first, mine2=mine2, mine3=mine3):
                here = pl.ds(j * size, size)
                got = rcv3[g][t, :, here].astype(jnp.int32).astype(jnp.float32) * scr[g][2, t, :, here]
                total = keep[g][t, mine2, mine3, :, here] + got
                low, high = total[:8], total[8:]
                snd4[g][t, :, here] = jnp.where(core == 0, high, low)
                there = pl.ds(pl.multiple_of(core * HALF + first + j * size, 128), size)
                out_ref[step, rows, there] = out_ref[step, rows, there] - jnp.where(core == 0, low, high)
                return 0

            sweep(width // size, finish)
            launch(t, lambda t, g=g: [last_copy(g, t)])

    def fifth(t):
        step, rows = t // 4, pl.ds(pl.multiple_of((t % 4) * 8, 8), 8)
        for g, (first, width, tiles) in enumerate(GROUPS):
            last_copy(g, t).wait_recv()
            there = pl.ds(pl.multiple_of((1 - core) * HALF + first, 128), width)
            out_ref[step, rows, there] = out_ref[step, rows, there] - rcv4[g][t]
        out_copy(t).start()

    def turn(i, _):
        def during(lag, body):
            @pl.when((i >= lag) & (i < lag + CHUNKS))
            def _():
                body(i - lag)

        @pl.when(i < LAG)
        def _():
            during(3, spread_3)
            during(2, spread_2)
            during(1, spread_1)
            during(0, spread_0)

        @pl.when(i == 0)
        def _():
            for j in range(4):
                remote_b(j).start()
            stiff_copy.start()
            mine_copy.wait()
            mask_copy.wait_recv()

        def own_slice(j):
            local_b(j).wait()
            mask_slice(0, mask_ref, j)

        def other_slice(j):
            remote_b(j).wait_recv()
            mask_slice(1, mask2, j)

        @pl.when(i < 3)
        def _():
            own_slice(i)

        @pl.when(i == 0)
        def _():
            own_slice(3)

        @pl.when((i >= 2) & (i < 4))
        def _():
            other_slice(i - 2)

        during(LAG, product)

        @pl.when(i >= LAG)
        def _():
            during(0, spread_0)
            during(1, spread_1)
            during(2, spread_2)
            during(3, spread_3)

        @pl.when(i == LAG + 3)
        def _():
            stiff_copy.wait()

        during(LAG + 1, second)
        during(LAG + 2, third)
        during(LAG + 3, fourth)
        during(LAG + 4, fifth)
        return 0

    lax.fori_loop(0, CHUNKS + LAG + 4, turn, 0)

    mask_copy.wait_send()
    for i in range(4):
        remote_b(i).wait_send()

    def written(t, _):
        out_copy(t).wait()
        return 0

    lax.fori_loop(0, CHUNKS, written, 0)

    def drain(t, _):
        for stage in range(3):
            for g in range(3):
                for copy in sum_copy(stage, g, t):
                    copy.wait_send()
        for p in range(2):
            for copy in (*scatters(p, t), *gathers(p, t), cross(p, t), twin_a(p, t)):
                copy.wait_send()
        for g in range(3):
            last_copy(g, t).wait_send()
        return 0

    lax.fori_loop(CHUNKS - SENDS, CHUNKS, drain, 0)


def shards(interior, tile_mask, owner, stiffness):
    cand = pick(owner, interior, tile_mask)
    widths = [width for _, width, _ in GROUPS]

    def each(dtype, *lead):
        return tuple(pltpu.VMEM((*lead, width), dtype) for width in widths)

    f32, i16, bf16 = jnp.float32, jnp.int16, jnp.bfloat16
    dma = pltpu.SemaphoreType.DMA
    result = pl.pallas_call(
        main_kernel,
        out_shape=jax.ShapeDtypeStruct(stiffness.shape, f32),
        in_specs=[
            pl.BlockSpec(memory_space=pl.ANY),
            pl.BlockSpec(memory_space=pltpu.VMEM),
            pl.BlockSpec(memory_space=pl.ANY),
            pl.BlockSpec(memory_space=pl.ANY),
        ],
        out_specs=pl.BlockSpec(memory_space=pl.ANY),
        scratch_shapes=[
            pltpu.VMEM((STEPS, 32, 2 * HALF), f32),
            pltpu.VMEM((CHUNKS, 2, 16, DEPTH), bf16),
            pltpu.VMEM((2 * DEPTH, HALF), bf16),
            pltpu.VMEM((CHUNKS, 2, 8, 16, DEPTH), bf16),
            pltpu.VMEM((CHUNKS, 3, 2, 16, DEPTH), bf16),
            pltpu.VMEM((CHUNKS, 2, 16, DEPTH), bf16),
            pltpu.VMEM((CHUNKS, 2, 16, DEPTH), bf16),
            pltpu.VMEM((16, 128), jnp.int32),
            each(f32, CHUNKS, 2, 2, 16),
            each(i16, CHUNKS, 2, 2, 16),
            each(i16, CHUNKS, 2, 2, 16),
            each(i16, CHUNKS, 2, 16),
            each(i16, CHUNKS, 2, 16),
            each(i16, CHUNKS, 16),
            each(i16, CHUNKS, 16),
            each(f32, CHUNKS, 8),
            each(f32, CHUNKS, 8),
            each(f32, 3, CHUNKS, 1),
            each(f32, 3, CHUNKS, 1),
            dma((2, 3, SENDS)), dma((2, 3, SLOTS)), dma((2, SENDS)), dma((2, SLOTS)),
            dma((2, 3, SENDS)), dma((2, 3, SLOTS)), dma((2, SENDS)), dma((2, SLOTS)),
            dma((3, 3, SENDS)), dma((3, 3, SLOTS)),
            dma((3, 3, SENDS)), dma((3, 3, SLOTS)),
            dma((3, SENDS)), dma((3, SLOTS)),
            dma((4,)), dma((4,)), dma((4,)),
            dma((1,)), dma((1,)), dma((1,)), dma((1,)), dma((CHUNKS,)),
        ],
        compiler_params=pltpu.CompilerParams(
            collective_id=0, has_side_effects=True, vmem_limit_bytes=62 * 1024 * 1024
        ),
    )(interior, tile_mask, cand, stiffness)
    return hand_over(result)


def solution(mesh):
    placed = (P("wide", "narrow"), P("wide", "narrow"), P(), P(None, "wide", "narrow"))
    return jax.shard_map(
        shards, mesh=mesh, in_specs=placed, out_specs=P(None, "wide", "narrow"), check_vma=False
    )
```
